32 devices in a mesh: grp: 4 (over z), loc: 2 (over x), tp: 4 (over y, core).
Axes of the slice: x: 2, y: 2, z: 4, core: 2. Of those that a mesh axis runs over, the one named last changes fastest.
Arguments:
- resid_in: bfloat16 [256, 4096], P(('grp', 'loc'), 'tp'), may hold values from -140 to 140
- attn_heads: bfloat16 [256, 16384], P('grp', 'loc'), may hold values from -6 to 6
- out_proj: bfloat16 [16384, 4096], P('loc', 'tp'), may hold values from -0.046875 to 0.046875
- norm_gain: float32 [4096], P('tp'), may hold values from 0.25 to 1.75
- expert_ids: int32 [256, 8], P(('grp', 'loc')), may hold values from 0 to 7, as said below
- gate_scores: int32 [256, 8], P(('grp', 'loc')), may hold values from 1 to 1023
- w_gate: bfloat16 [8, 4096, 1024], P(('grp', 'loc'), 'tp'), may hold values from -0.09375 to 0.09375
- w_up: bfloat16 [8, 4096, 1024], P(('grp', 'loc'), 'tp'), may hold values from -0.09375 to 0.09375
- w_down: bfloat16 [8, 1024, 4096], P(('grp', 'loc'), None, 'tp'), may hold values from -0.1875 to 0.1875
Outputs:
- layer_out: bfloat16 [256, 4096], P(('grp', 'loc'), 'tp')
The draws below stay inside these ranges and needn't reach their ends.
Inputs may be any that keep to these rules, and one draw needn't show every extreme that they name: `expert_ids`: each row names 8 different experts: 2 in each of 4 different groups, expert e being in group e // 2. In each aligned block of 32 rows (the tokens of one grp and loc position) no group is named by more than 32 rows and no expert by more than 32 rows; in every block some group and some expert reach these bounds, and some expert reaches 32 in every block.
All inputs are finite; a program needn't handle non-finite values.
Results may differ from the reference program's by a relative error of at most 0.0095.
Values may be sent and summed in bfloat16 or wider, within the bound.
A program may use at most 64 MiB of HBM per device.

```python
import jax
import jax.numpy as jnp
from jax import lax

D = 4096
HEADS = 128
HEAD_DIM = 128
FF = 1024
TOPK = 8
KEEP = 4
PER = 2
TOK_DEV = 32
GROUPS = 4
PER_GROUP = 2
EXPERTS = 8
TOKENS = 256
SLOTS = 256
N_TP = 4


def draw_resid_in(key, part):
    key_base, key_rows, key_cols = jax.random.split(jax.random.fold_in(key, 11), 3)
    base = jnp.clip(jax.random.normal(key_base, (TOKENS, D), jnp.float32), -6.0, 6.0)
    row_power = jax.random.uniform(key_rows, (TOKENS, 1), jnp.float32, -0.5, 0.5)
    column = jnp.arange(D, dtype=jnp.float32) / D
    col_power = jax.random.uniform(key_cols, (D,), jnp.float32, -0.4, 0.4) + (column - 0.5) * 0.48
    return (base * 10.0 ** row_power * 10.0 ** col_power).astype(jnp.bfloat16)


def shuffle_row(row_key, values):
    return jax.random.permutation(row_key, values)


def local_shuffle(group_key):
    return jax.random.permutation(group_key, PER_GROUP)


def draw_expert_ids(key, part):
    spread = GROUPS // KEEP
    group_cap = min(TOK_DEV, 2 * TOK_DEV // spread)
    block_count = TOKENS // TOK_DEV
    key_hot, key_top, key_blocks = jax.random.split(jax.random.fold_in(key, 23), 3)
    top_group = jax.random.randint(key_top, (), 0, GROUPS)
    hotness = jnp.where(jnp.arange(GROUPS) == top_group, 4, jax.random.randint(key_hot, (GROUPS,), 0, 4))

    def one_block(block_key):
        key_pool, key_order, key_groups, key_local, key_columns = jax.random.split(block_key, 5)
        forced = jnp.zeros((group_cap,), jnp.int32)
        if spread > 1:
            residue_pool = jnp.repeat(jnp.arange(1, spread, dtype=jnp.int32), group_cap)
            residue_pool = jax.random.permutation(key_pool, residue_pool)[:TOK_DEV - group_cap]
            residue = jnp.concatenate([forced, residue_pool])
        else:
            residue = forced
        residue = jax.random.permutation(key_order, residue)
        ranking = hotness * GROUPS + jax.random.permutation(key_groups, GROUPS)
        group_order = jnp.argsort(-ranking, stable=True).astype(jnp.int32)
        chosen = group_order[residue[:, None] * KEEP + jnp.arange(KEEP, dtype=jnp.int32)[None, :]]
        same_residue = residue[:, None] == residue[None, :]
        earlier = jnp.arange(TOK_DEV)[:, None] > jnp.arange(TOK_DEV)[None, :]
        rank_inside = jnp.sum(jnp.logical_and(same_residue, earlier), axis=1).astype(jnp.int32)
        local_order = jax.vmap(local_shuffle)(jax.random.split(key_local, GROUPS)).astype(jnp.int32)
        turn_index = (rank_inside[:, None, None] + jnp.arange(PER, dtype=jnp.int32)[None, None, :]) % PER_GROUP
        local_pick = local_order[chosen[:, :, None], turn_index]
        experts = (chosen[:, :, None] * PER_GROUP + local_pick).reshape(TOK_DEV, KEEP * PER)
        column_keys = jax.random.split(key_columns, TOK_DEV)
        return jax.vmap(shuffle_row)(column_keys, experts)
    block_keys = jax.random.split(key_blocks, block_count)
    return jax.vmap(one_block)(block_keys).reshape(TOKENS, TOPK).astype(jnp.int32)


def plant(array, own_key, smallest, high):
    longest = array.shape.index(max(array.shape))
    spots = []
    for shift in (0, 1):
        where = [jax.random.randint(jax.random.fold_in(own_key, axis), (), 0, length) for axis, length in enumerate(array.shape)]
        where[longest] = (where[longest] + shift) % array.shape[longest]
        spots.append(tuple(where))
    return array.at[spots[0]].set(smallest).at[spots[1]].set(high)


def levels(stream_key, extent, cuts, least, largest):
    def one(position, blocks):
        heights = jax.random.uniform(jax.random.fold_in(jax.random.fold_in(stream_key, 6), position), (blocks,), jnp.float32, least / len(cuts), largest / len(cuts))
        return jnp.repeat(jnp.exp(heights), extent[position] // blocks).reshape((-1,) + (1,) * (len(extent) - position - 1))

    level = one(*cuts[0])
    for cut in cuts[1:]:
        level = level * one(*cut)
    return level


def normal_values(rng, extent, deviation, bound, pieces=(), held_as=jnp.bfloat16):
    values = deviation * jax.random.normal(rng, extent, jnp.float32)
    if pieces:
        values = values * levels(rng, extent, pieces, -0.22, 0.18)
    return jnp.clip(values, -bound, bound).astype(held_as)


def setup_inputs(seed: int = 0) -> dict:
    key_list = jax.random.split(jax.random.key(seed), 10)
    return {
        "resid_in": draw_resid_in(jax.random.fold_in(key_list[9], 71), 0),
        "attn_heads": normal_values(key_list[1], (TOKENS, HEADS * HEAD_DIM), 1.0, 6.0, ((0, 4), (1, 2))),
        "out_proj": normal_values(key_list[2], (HEADS * HEAD_DIM, D), (HEADS * HEAD_DIM) ** -0.5, 0.046875, ((0, 2), (1, 4))),
        "norm_gain": jnp.clip(1.0 + 0.15 * jax.random.normal(key_list[3], (D,), jnp.float32), 0.25, 1.75),
        "expert_ids": draw_expert_ids(jax.random.fold_in(key_list[9], 71), 0),
        "gate_scores": plant(jax.random.randint(key_list[5], (TOKENS, TOPK), 1, 1024), jax.random.fold_in(key_list[5], 1), 1, 1023).astype(jnp.int32),
        "w_gate": normal_values(key_list[6], (EXPERTS, D, FF), D ** -0.5, 0.09375, ((0, 8), (1, 4))),
        "w_up": normal_values(key_list[7], (EXPERTS, D, FF), D ** -0.5, 0.09375, ((0, 8), (1, 4))),
        "w_down": normal_values(key_list[8], (EXPERTS, FF, D), FF ** -0.5, 0.1875, ((0, 8), (2, 4))),
    }


route_scale = 2.5
norm_eps = 1e-06

def reference(resid_in, attn_heads, out_proj, norm_gain, expert_ids, gate_scores, w_gate, w_up, w_down):
    attn_out = jnp.dot(attn_heads, out_proj, preferred_element_type=jnp.float32)
    mixed = resid_in.astype(jnp.float32) + attn_out
    mean_square = lax.optimization_barrier(jnp.mean(mixed * mixed, axis=1, keepdims=True))
    normed = (mixed * lax.rsqrt(mean_square + norm_eps) * norm_gain).astype(jnp.bfloat16)
    scores = gate_scores.astype(jnp.float32)
    route_weight = route_scale * scores / lax.optimization_barrier(jnp.sum(scores, axis=1, keepdims=True))
    lane_width = D // N_TP

    def block_sum(inputs, weight):
        parts = jnp.einsum('snd,ndf->snf', inputs.reshape(SLOTS, N_TP, lane_width).astype(jnp.float32), weight.reshape(N_TP, lane_width, FF).astype(jnp.float32), precision=lax.Precision.HIGHEST)
        rounded = lax.optimization_barrier(parts.astype(jnp.bfloat16))
        return lax.optimization_barrier(jnp.sum(rounded.astype(jnp.float32), axis=1))

    def group_step(running, group_inputs):
        group_id, gate_group, up_group, down_group = group_inputs

        def expert_step(group_acc, inputs):
            local_id, gate_w, up_w, down_w = inputs
            expert = group_id * PER_GROUP + local_id
            hits = expert_ids == expert
            is_named = jnp.any(hits, axis=1)
            token_weight = lax.optimization_barrier(jnp.sum(jnp.where(hits, route_weight, 0.0), axis=1))
            picked = jnp.nonzero(is_named, size=SLOTS, fill_value=0)[0].astype(jnp.int32)
            valid = (jnp.arange(SLOTS, dtype=jnp.int32) < jnp.sum(is_named.astype(jnp.int32))).astype(jnp.float32)
            chosen_rows = normed[picked]
            gate_pre = block_sum(chosen_rows, gate_w)
            up_pre = block_sum(chosen_rows, up_w)
            active = (jax.nn.silu(gate_pre) * up_pre).astype(jnp.bfloat16)
            expert_out = jnp.dot(active, down_w, preferred_element_type=jnp.float32).astype(jnp.bfloat16)
            scaled = expert_out.astype(jnp.float32) * (token_weight[picked] * valid)[:, None]
            return (group_acc.at[picked].add(scaled), None)
        group_acc, _ = lax.scan(expert_step, jnp.zeros((TOKENS, D), jnp.float32), (jnp.arange(PER_GROUP, dtype=jnp.int32), gate_group, up_group, down_group))
        group_part = lax.optimization_barrier(group_acc.astype(jnp.bfloat16))
        return (running + group_part.astype(jnp.float32), None)
    running, _ = lax.scan(group_step, mixed, (jnp.arange(GROUPS, dtype=jnp.int32), w_gate.reshape(GROUPS, PER_GROUP, D, FF), w_up.reshape(GROUPS, PER_GROUP, D, FF), w_down.reshape(GROUPS, PER_GROUP, FF, D)))
    return running.astype(jnp.bfloat16)
```

```python
import functools

import jax
import jax.numpy as jnp
from jax import lax
from jax.experimental import pallas as pl
from jax.experimental.pallas import tpu as pltpu
from jax.sharding import PartitionSpec as P

MESH = pl.DeviceIdType.MESH
LANES = 128

D = 4096
KEEP = 4
PER = 2


route_scale = 2.5
norm_eps = 1e-06


def routed(resid_in, attn_heads, out_proj, norm_gain, expert_ids, gate_scores, w_gate, w_up, w_down):
    group_count = lax.axis_size("grp")
    local_count = lax.axis_size("loc")
    block_rows = resid_in.shape[0]
    lane_width = resid_in.shape[1]
    expert_total = group_count * local_count
    spread = group_count // KEEP
    group_cap = min(block_rows, 2 * block_rows // spread)
    expert_cap = PER * group_cap // local_count
    slot_count = expert_total * expert_cap
    attn_out = lax.psum_scatter(
        jnp.dot(attn_heads, out_proj, preferred_element_type=jnp.float32).astype(jnp.bfloat16),
        "loc",
        scatter_dimension=0,
        tiled=True,
    ).astype(jnp.float32)
    mixed = resid_in.astype(jnp.float32) + attn_out
    square_sum = lax.psum(jnp.sum(mixed * mixed, axis=1), "tp")
    inverse_rms = lax.rsqrt(square_sum / D + norm_eps)
    normed = (mixed * inverse_rms[:, None] * norm_gain).astype(jnp.bfloat16)
    scores = gate_scores.astype(jnp.float32)
    route_weight = route_scale * scores / jnp.sum(scores, axis=1, keepdims=True)
    expert_hit = (expert_ids[:, :, None] == jnp.arange(expert_total, dtype=jnp.int32)).astype(
        jnp.float32
    )
    named_expert = jnp.sum(expert_hit, axis=1)
    expert_weight = jnp.sum(expert_hit * route_weight[:, :, None], axis=1)
    earlier = (jnp.arange(block_rows)[:, None] > jnp.arange(block_rows)[None, :]).astype(
        jnp.float32
    )
    before = jnp.dot(earlier, named_expert, precision=lax.Precision.HIGHEST)
    position = jnp.sum(expert_hit * before[:, None, :], axis=2).astype(jnp.int32)
    slot_index = expert_ids * expert_cap + position
    slot_hit = (slot_index[:, :, None] == jnp.arange(slot_count, dtype=jnp.int32)).astype(
        jnp.float32
    )
    group_ids = expert_ids // local_count
    group_hit = (group_ids[:, :, None] == jnp.arange(group_count, dtype=jnp.int32)).astype(
        jnp.float32
    )
    group_named = jnp.minimum(jnp.sum(group_hit, axis=1), 1.0)
    group_before = jnp.dot(earlier, group_named, precision=lax.Precision.HIGHEST)
    group_place = group_named[:, :, None] * (
        group_before[:, :, None] == jnp.arange(group_cap, dtype=jnp.float32)
    ).astype(jnp.float32)
    expert_rank = jnp.where(named_expert > 0, before, -1.0).reshape(
        block_rows, group_count, local_count
    )
    slot_info = (
        jnp.einsum("rgc,rgl->gcl", group_place, expert_rank + 1.0, precision=lax.Precision.HIGHEST)
        - 1.0
    )
    placement = jnp.sum(slot_hit, axis=1).astype(jnp.bfloat16)
    outgoing = jnp.einsum("rs,rd->sd", placement, normed, preferred_element_type=jnp.float32)
    outgoing = outgoing.astype(jnp.bfloat16).reshape(
        group_count, local_count, expert_cap, lane_width
    )
    arrived = lax.all_to_all(
        lax.all_to_all(outgoing, "grp", split_axis=0, concat_axis=0, tiled=True),
        "loc",
        split_axis=1,
        concat_axis=1,
        tiled=True,
    )
    slot_rows = arrived.reshape(slot_count, lane_width)
    gate_part = jnp.dot(slot_rows, w_gate[0], preferred_element_type=jnp.float32)
    up_part = jnp.dot(slot_rows, w_up[0], preferred_element_type=jnp.float32)
    gate_pre, up_pre = (
        lax.psum(gate_part.astype(jnp.bfloat16), "tp").astype(jnp.float32),
        lax.psum(up_part.astype(jnp.bfloat16), "tp").astype(jnp.float32),
    )
    active = (jax.nn.silu(gate_pre) * up_pre).astype(jnp.bfloat16)
    expert_out = jnp.dot(active, w_down[0], preferred_element_type=jnp.float32).astype(jnp.bfloat16)
    out_blocks = expert_out.reshape(group_count, local_count, expert_cap, lane_width)
    slot_weight = jnp.einsum(
        "rgc,rgl->gcl",
        group_place,
        expert_weight.reshape(block_rows, group_count, local_count),
        precision=lax.Precision.HIGHEST,
    )
    rank_there, weight_there = (
        lax.all_to_all(slot_info, "grp", split_axis=0, concat_axis=0, tiled=True),
        lax.all_to_all(slot_weight, "grp", split_axis=0, concat_axis=0, tiled=True),
    )
    at_group = lax.all_to_all(out_blocks, "loc", split_axis=1, concat_axis=1, tiled=True)
    picks = (rank_there[:, :, :, None] == jnp.arange(expert_cap, dtype=jnp.float32)).astype(
        jnp.float32
    )
    picks = picks * weight_there[:, :, :, None]
    summed = jnp.einsum(
        "gclp,glpd->gcd", picks, at_group.astype(jnp.float32), precision=lax.Precision.HIGHEST
    ).astype(jnp.bfloat16)
    at_owner = lax.all_to_all(summed, "grp", split_axis=0, concat_axis=0, tiled=True)
    layer_out = mixed + jnp.einsum(
        "rgc,gcd->rd", group_place, at_owner.astype(jnp.float32), precision=lax.Precision.HIGHEST
    )
    return layer_out.astype(jnp.bfloat16)


def dense_kernel(
    sizes, resid, heads, proj, gain, ids, scores, w_gate, w_up, w_down, out,
    heads_v, proj_v, gate_v, up_v, down_v, rs_out, rs_in, mixed, rows, sq_out, sq_in, info,
    core_out, core_in, own, y_out, y_in, active, pair_out, pair_in, part_out, part_in,
    local_sem, send_sem, recv_sem,
):
    groups, tp_count, parts, out_parts = sizes
    block, width = resid.shape
    depth = heads.shape[1]
    ff = gate_v.shape[1]
    piece = width // parts
    out_piece = width // out_parts
    fpiece = ff // tp_count
    tall = groups * block
    g, l, t = lax.axis_index("grp"), lax.axis_index("loc"), lax.axis_index("tp")
    core, y = lax.rem(t, 2), t // 2
    core_peer = t + 1 - 2 * core
    y_peer = t + 2 - 4 * y
    diagonal = core_peer + 2 - 4 * y
    at_core, at_y, at_x = {"tp": core_peer}, {"tp": y_peer}, {"loc": 1 - l}

    def at_group(step):
        return {"grp": lax.rem(g + step + groups, groups)}

    barrier = pltpu.get_barrier_semaphore()
    friends = [{"tp": lax.rem(t + r, tp_count)} for r in range(1, tp_count)]
    friends += [at_group(d) for d in range(1, groups)]
    friends += [{**at_group(d), **at_x} for d in range(groups)]
    for friend in friends:
        pl.semaphore_signal(barrier, inc=1, device_id=friend, device_id_type=MESH)

    local_count = [0]

    def fetch(src, dst):
        copy = pltpu.make_async_copy(src, dst, local_sem.at[local_count[0]])
        local_count[0] += 1
        return copy

    started = []
    remote_count = [0]

    def send(src, dst, device):
        n = remote_count[0]
        remote_count[0] += 1
        copy = pltpu.make_async_remote_copy(
            src_ref=src, dst_ref=dst, send_sem=send_sem.at[n], recv_sem=recv_sem.at[n],
            device_id=device, device_id_type=MESH,
        )
        copy.start()
        started.append(copy)
        return copy

    get_heads = fetch(heads, heads_v)
    half = depth // 2
    get_proj = [
        [
            fetch(
                proj.at[pl.ds(k * half, half), pl.ds(c * piece, piece)],
                proj_v.at[c, pl.ds(k * half, half)],
            )
            for k in range(2)
        ]
        for c in range(parts)
    ]
    get_gate = fetch(w_gate.at[0], gate_v)
    get_up = fetch(w_up.at[0], up_v)
    get_down = fetch(w_down.at[0], down_v)
    get_heads.start()
    for c in range(min(2, parts)):
        for copy in get_proj[c]:
            copy.start()

    lane = lax.broadcasted_iota(jnp.int32, (block, LANES), 1)
    score = scores[...].astype(jnp.float32)
    score = route_scale * score / jnp.sum(score, axis=1, keepdims=True)
    weights = jnp.zeros((block, LANES), jnp.float32)
    for k in range(ids.shape[1]):
        weights += jnp.where(ids[:, k : k + 1] == lane, score[:, k : k + 1], 0.0)

    rs, spread, forward = {}, {}, {}
    keep = [None] * parts
    square = [jnp.zeros((block, 1), jnp.float32)]

    def settle(c):
        columns = pl.ds(c * piece, piece)
        rs[c].wait_recv()
        total = resid[:, columns].astype(jnp.float32) + (keep[c] + rs_in[c].astype(jnp.float32))
        mixed[:, columns] = total
        square[0] += jnp.sum(total * total, axis=1, keepdims=True)
        rows[0, 0, :, columns] = (total * gain[:, columns]).astype(jnp.bfloat16)
        mine = rows.at[0, 0, :, columns]
        forward[c, 0] = send(mine, rows.at[1, 0, :, columns], at_x)
        for d in range(groups - 1, 0, -1):
            spread[c, d] = send(mine, rows.at[0, d, :, columns], at_group(d))

    def pass_on(c):
        columns = pl.ds(c * piece, piece)
        for d in range(1, groups):
            spread[c, d].wait_recv()
            here = rows.at[0, d, :, columns]
            forward[c, d] = send(here, rows.at[1, d, :, columns], at_x)

    for c in range(parts):
        if c == 0:
            get_heads.wait()
        for copy in get_proj[c]:
            copy.wait()
        if c + 2 < parts:
            for copy in get_proj[c + 2]:
                copy.start()
        if c + 2 == parts or parts == 1:
            get_gate.start()
            get_up.start()
            get_down.start()
        share = jnp.dot(heads_v[...], proj_v[c], preferred_element_type=jnp.float32)
        low, high = share[:block], share[block:]
        keep[c] = jnp.where(l == 0, low, high)
        rs_out[c] = jnp.where(l == 0, high, low).astype(jnp.bfloat16)
        if c == 0:
            pl.semaphore_wait(barrier, len(friends))
        rs[c] = send(rs_out.at[c], rs_in.at[c], at_x)
        if c >= 1:
            settle(c - 1)
        if c >= 2:
            pass_on(c - 2)
    settle(parts - 1)

    sq_out[...] = jnp.broadcast_to(square[0], sq_out.shape)
    sums = [
        send(sq_out, sq_in.at[r - 1], {"tp": lax.rem(t + r, tp_count)})
        for r in range(1, tp_count)
    ]
    if parts >= 2:
        pass_on(parts - 2)
    pass_on(parts - 1)
    total_square = sq_out[...]
    for r, copy in enumerate(sums):
        copy.wait_recv()
        total_square += sq_in[r]
    inverse = lax.rsqrt(total_square / (width * tp_count) + norm_eps)
    expert_count = ids.shape[1]
    info[0, 0] = jnp.where(lane < expert_count, weights, inverse)
    told = {}
    for d in range(groups):
        told[1, d] = send(info.at[0, 0], info.at[1, d], {**at_group(d), **at_x})
    for d in range(1, groups):
        told[0, d] = send(info.at[0, 0], info.at[0, d], at_group(d))

    get_gate.wait()
    get_up.wait()

    def pair(side, q):
        x = rows[side].reshape(tall, width)
        columns = pl.ds(pl.multiple_of(q * fpiece, fpiece), fpiece)
        return (
            jnp.dot(x, gate_v[:, columns], preferred_element_type=jnp.float32),
            jnp.dot(x, up_v[:, columns], preferred_element_type=jnp.float32),
        )

    over_core, over_y, from_y, from_core, relay = {}, {}, {}, {}, {}

    def give(side):
        if side == 1:
            for c in range(parts):
                for d in range(groups):
                    forward[c, d].wait_recv()
        for n, q in enumerate((diagonal, core_peer)):
            for m, value in enumerate(pair(side, q)):
                core_out[side, n, m] = value.astype(jnp.bfloat16)
            over_core[side, n] = send(core_out.at[side, n], core_in.at[side, n], at_core)

    def hold(side):
        for n, q in enumerate((y_peer, t)):
            for m, value in enumerate(pair(side, q)):
                own[side, n, m] = value

    def cross(side):
        over_core[side, 0].wait_recv()
        y_out[side] = (own[side, 0] + core_in[side, 0].astype(jnp.float32)).astype(jnp.bfloat16)
        over_y[side] = send(y_out.at[side], y_in.at[side], at_y)

    def activate(side):
        over_core[side, 1].wait_recv()
        kept = own[side, 1] + core_in[side, 1].astype(jnp.float32)
        for d in range(groups):
            if (side, d) in told:
                told[side, d].wait_recv()
        known = info[side].reshape(tall, LANES)
        known_lane = lax.broadcasted_iota(jnp.int32, (tall, LANES), 1)
        expert = g * 2 + l
        scale = known[:, expert_count : expert_count + 1]
        weight = jnp.sum(jnp.where(known_lane == expert, known, 0.0), axis=1, keepdims=True)
        over_y[side].wait_recv()
        pre = (kept + y_in[side].astype(jnp.float32)) * scale
        gate_pre, up_pre = pre[0], pre[1]
        value = gate_pre / (1.0 + jnp.exp(-gate_pre)) * up_pre * weight
        active[side, 0] = value.astype(jnp.bfloat16)
        from_y[side] = send(active.at[side, 0], active.at[side, 2], at_y)
        from_core[side] = send(active.at[side, 0], active.at[side, 1], at_core)

    def hand_over(side):
        from_y[side].wait_recv()
        relay[side] = send(active.at[side, 2], active.at[side, 3], at_core)

    def down(side, c):
        columns = pl.ds(c * out_piece, out_piece)
        total = None
        for n, q in enumerate((t, core_peer, y_peer, diagonal)):
            if c == 0 and n == 1:
                from_core[side].wait_recv()
            if c == 0 and n == 3:
                relay[side].wait_recv()
            part = jnp.dot(
                active[side, n],
                down_v[pl.ds(pl.multiple_of(q * fpiece, fpiece), fpiece), columns],
                preferred_element_type=jnp.float32,
            )
            total = part if total is None else total + part
        return total

    give(1)
    hold(1)
    give(0)
    cross(1)
    hold(0)
    cross(0)
    get_down.wait()
    activate(1)
    activate(0)
    hand_over(1)
    across, home = {}, {}
    for c in range(out_parts):
        pair_out[c] = down(1, c).astype(jnp.bfloat16)
        across[c] = send(pair_out.at[c], pair_in.at[c], at_x)
        if c == 0:
            hand_over(0)
    for c in range(out_parts):
        summed = down(0, c)
        across[c].wait_recv()
        summed += pair_in[c].astype(jnp.float32)
        part_out[c] = summed.astype(jnp.bfloat16).reshape(groups, block, out_piece)
        for d in range(1, groups):
            home[c, d] = send(part_out.at[c, d], part_in.at[c, d - 1], at_group(-d))
    for c in range(out_parts):
        columns = pl.ds(c * out_piece, out_piece)
        total = mixed[:, columns] + part_out[c, 0].astype(jnp.float32)
        for d in range(1, groups):
            home[c, d].wait_recv()
            total += part_in[c, d - 1].astype(jnp.float32)
        out[:, columns] = total.astype(out.dtype)
    for copy in started:
        copy.wait_send()


def dense(resid_in, attn_heads, out_proj, norm_gain, expert_ids, gate_scores, w_gate, w_up, w_down):
    groups, tp_count = lax.axis_size("grp"), lax.axis_size("tp")
    block, width = resid_in.shape
    heads_shape = attn_heads.shape
    ff = w_gate.shape[2]
    fpiece = ff // tp_count
    tall = groups * block
    parts, out_parts = 4, 2
    piece, out_piece = width // parts, width // out_parts
    bf16, f32 = jnp.bfloat16, jnp.float32
    local_copies = 4 + 2 * parts
    remote_copies = (
        parts + parts * (2 * groups - 1) + (tp_count - 1) + (2 * groups - 1) + 4 + 2 + 6
        + out_parts * groups
    )
    vmem = pl.BlockSpec(memory_space=pltpu.VMEM)
    anywhere = pl.BlockSpec(memory_space=pl.ANY)
    return pl.pallas_call(
        functools.partial(dense_kernel, (groups, tp_count, parts, out_parts)),
        out_shape=jax.ShapeDtypeStruct(resid_in.shape, bf16),
        in_specs=[vmem, anywhere, anywhere, vmem, vmem, vmem, anywhere, anywhere, anywhere],
        out_specs=vmem,
        scratch_shapes=[
            pltpu.VMEM(heads_shape, bf16),
            pltpu.VMEM((parts, heads_shape[1], piece), bf16),
            pltpu.VMEM((width, ff), bf16),
            pltpu.VMEM((width, ff), bf16),
            pltpu.VMEM((ff, width), bf16),
            pltpu.VMEM((parts, block, piece), bf16),
            pltpu.VMEM((parts, block, piece), bf16),
            pltpu.VMEM((block, width), f32),
            pltpu.VMEM((2, groups, block, width), bf16),
            pltpu.VMEM((block, LANES), f32),
            pltpu.VMEM((tp_count - 1, block, LANES), f32),
            pltpu.VMEM((2, groups, block, LANES), f32),
            pltpu.VMEM((2, 2, 2, tall, fpiece), bf16),
            pltpu.VMEM((2, 2, 2, tall, fpiece), bf16),
            pltpu.VMEM((2, 2, 2, tall, fpiece), f32),
            pltpu.VMEM((2, 2, tall, fpiece), bf16),
            pltpu.VMEM((2, 2, tall, fpiece), bf16),
            pltpu.VMEM((2, 4, tall, fpiece), bf16),
            pltpu.VMEM((out_parts, tall, out_piece), bf16),
            pltpu.VMEM((out_parts, tall, out_piece), bf16),
            pltpu.VMEM((out_parts, groups, block, out_piece), bf16),
            pltpu.VMEM((out_parts, groups - 1, block, out_piece), bf16),
            pltpu.SemaphoreType.DMA((local_copies,)),
            pltpu.SemaphoreType.DMA((remote_copies,)),
            pltpu.SemaphoreType.DMA((remote_copies,)),
        ],
        compiler_params=pltpu.CompilerParams(
            collective_id=0, has_side_effects=True, vmem_limit_bytes=52 * 1024 * 1024
        ),
    )(
        resid_in, attn_heads, out_proj, norm_gain.reshape(1, width), expert_ids, gate_scores,
        w_gate, w_up, w_down,
    )


def local(*arrays):
    expert_ids = arrays[4]
    expert_total = lax.axis_size("grp") * lax.axis_size("loc")
    if (
        expert_ids.shape[1] == expert_total
        and lax.axis_size("loc") == 2
        and lax.axis_size("tp") == 4
    ):
        return dense(*arrays)
    return routed(*arrays)


def solution(mesh):
    placed = (
        P(("grp", "loc"), "tp"),
        P("grp", "loc"),
        P("loc", "tp"),
        P("tp"),
        P(("grp", "loc"), None),
        P(("grp", "loc"), None),
        P(("grp", "loc"), "tp", None),
        P(("grp", "loc"), "tp", None),
        P(("grp", "loc"), None, "tp"),
    )
    return jax.shard_map(
        local, mesh=mesh, in_specs=placed, out_specs=P(("grp", "loc"), "tp"), check_vma=False
    )
```

```python
import functools

import jax
import jax.numpy as jnp
from jax import lax
from jax.experimental import pallas as pl
from jax.experimental.pallas import tpu as pltpu
from jax.sharding import PartitionSpec as P

MESH = pl.DeviceIdType.MESH
LANES = 128

D = 4096
KEEP = 4
PER = 2


route_scale = 2.5
norm_eps = 1e-06


def routed(resid_in, attn_heads, out_proj, norm_gain, expert_ids, gate_scores, w_gate, w_up, w_down):
    group_count = lax.axis_size("grp")
    local_count = lax.axis_size("loc")
    block_rows = resid_in.shape[0]
    lane_width = resid_in.shape[1]
    expert_total = group_count * local_count
    spread = group_count // KEEP
    group_cap = min(block_rows, 2 * block_rows // spread)
    expert_cap = PER * group_cap // local_count
    slot_count = expert_total * expert_cap
    attn_out = lax.psum_scatter(
        jnp.dot(attn_heads, out_proj, preferred_element_type=jnp.float32).astype(jnp.bfloat16),
        "loc",
        scatter_dimension=0,
        tiled=True,
    ).astype(jnp.float32)
    mixed = resid_in.astype(jnp.float32) + attn_out
    square_sum = lax.psum(jnp.sum(mixed * mixed, axis=1), "tp")
    inverse_rms = lax.rsqrt(square_sum / D + norm_eps)
    normed = (mixed * inverse_rms[:, None] * norm_gain).astype(jnp.bfloat16)
    scores = gate_scores.astype(jnp.float32)
    route_weight = route_scale * scores / jnp.sum(scores, axis=1, keepdims=True)
    expert_hit = (expert_ids[:, :, None] == jnp.arange(expert_total, dtype=jnp.int32)).astype(
        jnp.float32
    )
    named_expert = jnp.sum(expert_hit, axis=1)
    expert_weight = jnp.sum(expert_hit * route_weight[:, :, None], axis=1)
    earlier = (jnp.arange(block_rows)[:, None] > jnp.arange(block_rows)[None, :]).astype(
        jnp.float32
    )
    before = jnp.dot(earlier, named_expert, precision=lax.Precision.HIGHEST)
    position = jnp.sum(expert_hit * before[:, None, :], axis=2).astype(jnp.int32)
    slot_index = expert_ids * expert_cap + position
    slot_hit = (slot_index[:, :, None] == jnp.arange(slot_count, dtype=jnp.int32)).astype(
        jnp.float32
    )
    group_ids = expert_ids // local_count
    group_hit = (group_ids[:, :, None] == jnp.arange(group_count, dtype=jnp.int32)).astype(
        jnp.float32
    )
    group_named = jnp.minimum(jnp.sum(group_hit, axis=1), 1.0)
    group_before = jnp.dot(earlier, group_named, precision=lax.Precision.HIGHEST)
    group_place = group_named[:, :, None] * (
        group_before[:, :, None] == jnp.arange(group_cap, dtype=jnp.float32)
    ).astype(jnp.float32)
    expert_rank = jnp.where(named_expert > 0, before, -1.0).reshape(
        block_rows, group_count, local_count
    )
    slot_info = (
        jnp.einsum("rgc,rgl->gcl", group_place, expert_rank + 1.0, precision=lax.Precision.HIGHEST)
        - 1.0
    )
    placement = jnp.sum(slot_hit, axis=1).astype(jnp.bfloat16)
    outgoing = jnp.einsum("rs,rd->sd", placement, normed, preferred_element_type=jnp.float32)
    outgoing = outgoing.astype(jnp.bfloat16).reshape(
        group_count, local_count, expert_cap, lane_width
    )
    arrived = lax.all_to_all(
        lax.all_to_all(outgoing, "grp", split_axis=0, concat_axis=0, tiled=True),
        "loc",
        split_axis=1,
        concat_axis=1,
        tiled=True,
    )
    slot_rows = arrived.reshape(slot_count, lane_width)
    gate_part = jnp.dot(slot_rows, w_gate[0], preferred_element_type=jnp.float32)
    up_part = jnp.dot(slot_rows, w_up[0], preferred_element_type=jnp.float32)
    gate_pre, up_pre = (
        lax.psum(gate_part.astype(jnp.bfloat16), "tp").astype(jnp.float32),
        lax.psum(up_part.astype(jnp.bfloat16), "tp").astype(jnp.float32),
    )
    active = (jax.nn.silu(gate_pre) * up_pre).astype(jnp.bfloat16)
    expert_out = jnp.dot(active, w_down[0], preferred_element_type=jnp.float32).astype(jnp.bfloat16)
    out_blocks = expert_out.reshape(group_count, local_count, expert_cap, lane_width)
    slot_weight = jnp.einsum(
        "rgc,rgl->gcl",
        group_place,
        expert_weight.reshape(block_rows, group_count, local_count),
        precision=lax.Precision.HIGHEST,
    )
    rank_there, weight_there = (
        lax.all_to_all(slot_info, "grp", split_axis=0, concat_axis=0, tiled=True),
        lax.all_to_all(slot_weight, "grp", split_axis=0, concat_axis=0, tiled=True),
    )
    at_group = lax.all_to_all(out_blocks, "loc", split_axis=1, concat_axis=1, tiled=True)
    picks = (rank_there[:, :, :, None] == jnp.arange(expert_cap, dtype=jnp.float32)).astype(
        jnp.float32
    )
    picks = picks * weight_there[:, :, :, None]
    summed = jnp.einsum(
        "gclp,glpd->gcd", picks, at_group.astype(jnp.float32), precision=lax.Precision.HIGHEST
    ).astype(jnp.bfloat16)
    at_owner = lax.all_to_all(summed, "grp", split_axis=0, concat_axis=0, tiled=True)
    layer_out = mixed + jnp.einsum(
        "rgc,gcd->rd", group_place, at_owner.astype(jnp.float32), precision=lax.Precision.HIGHEST
    )
    return layer_out.astype(jnp.bfloat16)


def dense_kernel(
    sizes, resid_hbm, heads, proj, gain_hbm, ids_hbm, scores_hbm, w_gate, w_up, w_down, out,
    resid, gain, ids, scores, heads_v, proj_v, gate_v, up_v, down_v, rs_out, rs_in, mixed, rows, sq_out, sq_in, info,
    core_out, core_in, own, y_out, y_in, active, kept_down, pair_out, pair_in, part_out, part_in,
    local_sem, send_sem, recv_sem,
):
    groups, tp_count, parts, out_parts = sizes
    block, width = resid.shape
    depth = heads.shape[1]
    ff = gate_v.shape[1]
    piece = width // parts
    out_piece = width // out_parts
    fpiece = ff // tp_count
    tall = groups * block
    g, l, t = lax.axis_index("grp"), lax.axis_index("loc"), lax.axis_index("tp")
    core, y = lax.rem(t, 2), t // 2
    core_peer = t + 1 - 2 * core
    y_peer = t + 2 - 4 * y
    diagonal = core_peer + 2 - 4 * y
    at_core, at_y, at_x = {"tp": core_peer}, {"tp": y_peer}, {"loc": 1 - l}

    def at_group(step):
        return {"grp": lax.rem(g + step + groups, groups)}

    barrier = pltpu.get_barrier_semaphore()
    friends = [{"tp": lax.rem(t + r, tp_count)} for r in range(1, tp_count)]
    friends += [at_group(d) for d in range(1, groups)]
    friends += [{**at_group(d), **at_x} for d in range(groups)]
    for friend in friends:
        pl.semaphore_signal(barrier, inc=1, device_id=friend, device_id_type=MESH)

    local_count = [0]

    def fetch(src, dst):
        copy = pltpu.make_async_copy(src, dst, local_sem.at[local_count[0]])
        local_count[0] += 1
        return copy

    started = []
    remote_count = [0]

    def send(src, dst, device):
        n = remote_count[0]
        remote_count[0] += 1
        copy = pltpu.make_async_remote_copy(
            src_ref=src, dst_ref=dst, send_sem=send_sem.at[n], recv_sem=recv_sem.at[n],
            device_id=device, device_id_type=MESH,
        )
        copy.start()
        started.append(copy)
        return copy

    get_heads = fetch(heads, heads_v)
    half = depth // 2
    get_proj = [
        fetch(
            proj.at[pl.ds(k * half, half), pl.ds(c * piece, piece)],
            proj_v.at[c, pl.ds(k * half, half)],
        )
        for c in range(parts)
        for k in range(2)
    ]
    get_small = [
        fetch(ids_hbm, ids), fetch(scores_hbm, scores), fetch(gain_hbm, gain),
        fetch(resid_hbm, resid),
    ]
    get_gate = fetch(w_gate.at[0], gate_v)
    get_up = fetch(w_up.at[0], up_v)
    get_down = fetch(w_down.at[0], down_v)
    queue = get_proj + [get_gate, get_up, get_down]
    for copy in [get_heads] + queue[:2] + get_small + queue[2:3]:
        copy.start()
    for copy in get_small:
        copy.wait()

    lane = lax.broadcasted_iota(jnp.int32, (block, LANES), 1)
    square_row = lax.broadcasted_iota(jnp.int32, (block, block), 0)
    square_lane = lax.broadcasted_iota(jnp.int32, (block, block), 1)
    expert_count = ids.shape[0]

    def upright(row):
        return jnp.sum(jnp.where(square_row == square_lane, row, 0.0), axis=1, keepdims=True)

    score = scores[...].astype(jnp.float32)
    score = route_scale * score / jnp.sum(score, axis=0, keepdims=True)
    named = ids[...].astype(jnp.float32)
    weights = jnp.zeros((block, LANES), jnp.float32)
    for k in range(expert_count):
        column = upright(named[k : k + 1]).astype(jnp.int32)
        weights += jnp.where(column == lane, upright(score[k : k + 1]), 0.0)

    rs, spread, forward = {}, {}, {}
    keep = [None] * parts
    square = [jnp.zeros((block, 1), jnp.float32)]

    def settle(c):
        columns = pl.ds(c * piece, piece)
        rs[c].wait_recv()
        total = resid[:, columns].astype(jnp.float32) + (keep[c] + rs_in[c].astype(jnp.float32))
        mixed[:, columns] = total
        square[0] += jnp.sum(total * total, axis=1, keepdims=True)
        rows[0, 0, :, columns] = (total * gain[:, columns]).astype(jnp.bfloat16)
        mine = rows.at[0, 0, :, columns]
        forward[c, 0] = send(mine, rows.at[1, 0, :, columns], at_x)
        for d in range(groups - 1, 0, -1):
            spread[c, d] = send(mine, rows.at[0, d, :, columns], at_group(d))

    def pass_on(c):
        columns = pl.ds(c * piece, piece)
        for d in range(1, groups):
            spread[c, d].wait_recv()
            here = rows.at[0, d, :, columns]
            forward[c, d] = send(here, rows.at[1, d, :, columns], at_x)

    for c in range(parts):
        share = None
        for k in range(2):
            n = 2 * c + k
            queue[n].wait()
            if n + 3 < len(queue):
                queue[n + 3].start()
            if n == 0:
                get_heads.wait()
            term = jnp.dot(
                heads_v[:, pl.ds(k * half, half)],
                proj_v[c, pl.ds(k * half, half)],
                preferred_element_type=jnp.float32,
            )
            share = term if share is None else share + term
        low, high = share[:block], share[block:]
        keep[c] = jnp.where(l == 0, low, high)
        rs_out[c] = jnp.where(l == 0, high, low).astype(jnp.bfloat16)
        if c == 0:
            pl.semaphore_wait(barrier, len(friends))
        rs[c] = send(rs_out.at[c], rs_in.at[c], at_x)
        if c >= 1:
            settle(c - 1)
    settle(parts - 1)

    sq_out[...] = jnp.broadcast_to(square[0], sq_out.shape)
    sums = [
        send(sq_out, sq_in.at[r - 1], {"tp": lax.rem(t + r, tp_count)})
        for r in range(1, tp_count)
    ]
    for c in range(parts):
        pass_on(c)

    told = {}

    def tell():
        total_square = sq_out[...]
        for r, copy in enumerate(sums):
            copy.wait_recv()
            total_square += sq_in[r]
        inverse = lax.rsqrt(total_square / (width * tp_count) + norm_eps)
        info[0, 0] = jnp.where(lane < expert_count, weights, inverse)
        for d in range(groups):
            told[1, d] = send(info.at[0, 0], info.at[1, d], {**at_group(d), **at_x})
        for d in range(1, groups):
            told[0, d] = send(info.at[0, 0], info.at[0, d], at_group(d))

    get_gate.wait()
    get_up.wait()

    def pair(side, q):
        x = rows[side].reshape(tall, width)
        columns = pl.ds(pl.multiple_of(q * fpiece, fpiece), fpiece)
        return (
            jnp.dot(x, gate_v[:, columns], preferred_element_type=jnp.float32),
            jnp.dot(x, up_v[:, columns], preferred_element_type=jnp.float32),
        )

    over_core, over_y, from_y, from_core, relay = {}, {}, {}, {}, {}

    def give(side):
        if side == 1:
            for c in range(parts):
                for d in range(groups):
                    forward[c, d].wait_recv()
        for n, q in enumerate((diagonal, core_peer)):
            for m, value in enumerate(pair(side, q)):
                core_out[side, n, m] = value.astype(jnp.bfloat16)
            over_core[side, n] = send(core_out.at[side, n], core_in.at[side, n], at_core)

    def hold(side):
        for n, q in enumerate((y_peer, t)):
            for m, value in enumerate(pair(side, q)):
                own[side, n, m] = value

    def cross(side):
        over_core[side, 0].wait_recv()
        y_out[side] = (own[side, 0] + core_in[side, 0].astype(jnp.float32)).astype(jnp.bfloat16)
        over_y[side] = send(y_out.at[side], y_in.at[side], at_y)

    def activate(side):
        over_core[side, 1].wait_recv()
        kept = own[side, 1] + core_in[side, 1].astype(jnp.float32)
        for d in range(groups):
            if (side, d) in told:
                told[side, d].wait_recv()
        known = info[side].reshape(tall, LANES)
        known_lane = lax.broadcasted_iota(jnp.int32, (tall, LANES), 1)
        expert = g * 2 + l
        scale = known[:, expert_count : expert_count + 1]
        weight = jnp.sum(jnp.where(known_lane == expert, known, 0.0), axis=1, keepdims=True)
        over_y[side].wait_recv()
        pre = (kept + y_in[side].astype(jnp.float32)) * scale
        gate_pre, up_pre = pre[0], pre[1]
        value = gate_pre / (1.0 + jnp.exp(-gate_pre)) * up_pre * weight
        active[side, 0] = value.astype(jnp.bfloat16)
        from_y[side] = send(active.at[side, 0], active.at[side, 2], at_y)
        from_core[side] = send(active.at[side, 0], active.at[side, 1], at_core)

    def hand_over(side):
        from_y[side].wait_recv()
        relay[side] = send(active.at[side, 2], active.at[side, 3], at_core)

    def down(side, c):
        columns = pl.ds(c * out_piece, out_piece)
        total = None
        for n, q in enumerate((t, core_peer, y_peer, diagonal)):
            if c == 0 and n == 1:
                from_core[side].wait_recv()
            if c == 0 and n == 3:
                relay[side].wait_recv()
            part = jnp.dot(
                active[side, n],
                down_v[pl.ds(pl.multiple_of(q * fpiece, fpiece), fpiece), columns],
                preferred_element_type=jnp.float32,
            )
            total = part if total is None else total + part
        return total

    give(0)
    tell()
    hold(0)
    cross(0)
    give(1)
    hold(1)
    cross(1)
    get_down.wait()
    activate(0)
    hand_over(0)
    activate(1)
    for c in range(out_parts):
        kept_down[c] = down(0, c)
    hand_over(1)
    across, home = {}, {}
    for c in range(out_parts):
        pair_out[c] = down(1, c).astype(jnp.bfloat16)
        across[c] = send(pair_out.at[c], pair_in.at[c], at_x)
    for c in range(out_parts):
        across[c].wait_recv()
        summed = kept_down[c] + pair_in[c].astype(jnp.float32)
        part_out[c] = summed.astype(jnp.bfloat16).reshape(groups, block, out_piece)
        for d in range(1, groups):
            home[c, d] = send(part_out.at[c, d], part_in.at[c, d - 1], at_group(-d))
    for c in range(out_parts):
        columns = pl.ds(c * out_piece, out_piece)
        total = mixed[:, columns] + part_out[c, 0].astype(jnp.float32)
        for d in range(1, groups):
            home[c, d].wait_recv()
            total += part_in[c, d - 1].astype(jnp.float32)
        out[:, columns] = total.astype(out.dtype)
    for copy in started:
        copy.wait_send()


def dense(resid_in, attn_heads, out_proj, norm_gain, expert_ids, gate_scores, w_gate, w_up, w_down):
    groups, tp_count = lax.axis_size("grp"), lax.axis_size("tp")
    block, width = resid_in.shape
    heads_shape = attn_heads.shape
    ff = w_gate.shape[2]
    fpiece = ff // tp_count
    tall = groups * block
    parts, out_parts = 4, 4
    piece, out_piece = width // parts, width // out_parts
    bf16, f32 = jnp.bfloat16, jnp.float32
    local_copies = 8 + 2 * parts
    remote_copies = (
        parts + parts * (2 * groups - 1) + (tp_count - 1) + (2 * groups - 1) + 4 + 2 + 6
        + out_parts * groups
    )
    vmem = pl.BlockSpec(memory_space=pltpu.VMEM)
    return pl.pallas_call(
        functools.partial(dense_kernel, (groups, tp_count, parts, out_parts)),
        out_shape=jax.ShapeDtypeStruct(resid_in.shape, bf16),
        in_specs=[pl.BlockSpec(memory_space=pltpu.HBM)] * 9,
        out_specs=vmem,
        scratch_shapes=[
            pltpu.VMEM((block, width), bf16),
            pltpu.VMEM((1, width), f32),
            pltpu.VMEM(expert_ids.shape[::-1], jnp.int32),
            pltpu.VMEM(gate_scores.shape[::-1], jnp.int32),
            pltpu.VMEM(heads_shape, bf16),
            pltpu.VMEM((parts, heads_shape[1], piece), bf16),
            pltpu.VMEM((width, ff), bf16),
            pltpu.VMEM((width, ff), bf16),
            pltpu.VMEM((ff, width), bf16),
            pltpu.VMEM((parts, block, piece), bf16),
            pltpu.VMEM((parts, block, piece), bf16),
            pltpu.VMEM((block, width), f32),
            pltpu.VMEM((2, groups, block, width), bf16),
            pltpu.VMEM((block, LANES), f32),
            pltpu.VMEM((tp_count - 1, block, LANES), f32),
            pltpu.VMEM((2, groups, block, LANES), f32),
            pltpu.VMEM((2, 2, 2, tall, fpiece), bf16),
            pltpu.VMEM((2, 2, 2, tall, fpiece), bf16),
            pltpu.VMEM((2, 2, 2, tall, fpiece), f32),
            pltpu.VMEM((2, 2, tall, fpiece), bf16),
            pltpu.VMEM((2, 2, tall, fpiece), bf16),
            pltpu.VMEM((2, 4, tall, fpiece), bf16),
            pltpu.VMEM((out_parts, tall, out_piece), f32),
            pltpu.VMEM((out_parts, tall, out_piece), bf16),
            pltpu.VMEM((out_parts, tall, out_piece), bf16),
            pltpu.VMEM((out_parts, groups, block, out_piece), bf16),
            pltpu.VMEM((out_parts, groups - 1, block, out_piece), bf16),
            pltpu.SemaphoreType.DMA((local_copies,)),
            pltpu.SemaphoreType.DMA((remote_copies,)),
            pltpu.SemaphoreType.DMA((remote_copies,)),
        ],
        compiler_params=pltpu.CompilerParams(
            collective_id=0, has_side_effects=True, vmem_limit_bytes=64 * 1024 * 1024
        ),
    )(
        resid_in, attn_heads, out_proj, norm_gain.reshape(1, width), expert_ids.T, gate_scores.T,
        w_gate, w_up, w_down,
    )


def local(*arrays):
    expert_ids = arrays[4]
    expert_total = lax.axis_size("grp") * lax.axis_size("loc")
    if (
        expert_ids.shape[1] == expert_total
        and lax.axis_size("loc") == 2
        and lax.axis_size("tp") == 4
    ):
        return dense(*arrays)
    return routed(*arrays)


def solution(mesh):
    placed = (
        P(("grp", "loc"), "tp"),
        P("grp", "loc"),
        P("loc", "tp"),
        P("tp"),
        P(("grp", "loc"), None),
        P(("grp", "loc"), None),
        P(("grp", "loc"), "tp", None),
        P(("grp", "loc"), "tp", None),
        P(("grp", "loc"), None, "tp"),
    )
    return jax.shard_map(
        local, mesh=mesh, in_specs=placed, out_specs=P(("grp", "loc"), "tp"), check_vma=False
    )
```

```python
import functools

import jax
import jax.numpy as jnp
from jax import lax
from jax.experimental import pallas as pl
from jax.experimental.pallas import tpu as pltpu
from jax.sharding import PartitionSpec as P

MESH = pl.DeviceIdType.MESH
LANES = 128

D = 4096
KEEP = 4
PER = 2


route_scale = 2.5
norm_eps = 1e-06


def routed(resid_in, attn_heads, out_proj, norm_gain, expert_ids, gate_scores, w_gate, w_up, w_down):
    group_count = lax.axis_size("grp")
    local_count = lax.axis_size("loc")
    block_rows = resid_in.shape[0]
    lane_width = resid_in.shape[1]
    expert_total = group_count * local_count
    spread = group_count // KEEP
    group_cap = min(block_rows, 2 * block_rows // spread)
    expert_cap = PER * group_cap // local_count
    slot_count = expert_total * expert_cap
    attn_out = lax.psum_scatter(
        jnp.dot(attn_heads, out_proj, preferred_element_type=jnp.float32).astype(jnp.bfloat16),
        "loc",
        scatter_dimension=0,
        tiled=True,
    ).astype(jnp.float32)
    mixed = resid_in.astype(jnp.float32) + attn_out
    square_sum = lax.psum(jnp.sum(mixed * mixed, axis=1), "tp")
    inverse_rms = lax.rsqrt(square_sum / D + norm_eps)
    normed = (mixed * inverse_rms[:, None] * norm_gain).astype(jnp.bfloat16)
    scores = gate_scores.astype(jnp.float32)
    route_weight = route_scale * scores / jnp.sum(scores, axis=1, keepdims=True)
    expert_hit = (expert_ids[:, :, None] == jnp.arange(expert_total, dtype=jnp.int32)).astype(
        jnp.float32
    )
    named_expert = jnp.sum(expert_hit, axis=1)
    expert_weight = jnp.sum(expert_hit * route_weight[:, :, None], axis=1)
    earlier = (jnp.arange(block_rows)[:, None] > jnp.arange(block_rows)[None, :]).astype(
        jnp.float32
    )
    before = jnp.dot(earlier, named_expert, precision=lax.Precision.HIGHEST)
    position = jnp.sum(expert_hit * before[:, None, :], axis=2).astype(jnp.int32)
    slot_index = expert_ids * expert_cap + position
    slot_hit = (slot_index[:, :, None] == jnp.arange(slot_count, dtype=jnp.int32)).astype(
        jnp.float32
    )
    group_ids = expert_ids // local_count
    group_hit = (group_ids[:, :, None] == jnp.arange(group_count, dtype=jnp.int32)).astype(
        jnp.float32
    )
    group_named = jnp.minimum(jnp.sum(group_hit, axis=1), 1.0)
    group_before = jnp.dot(earlier, group_named, precision=lax.Precision.HIGHEST)
    group_place = group_named[:, :, None] * (
        group_before[:, :, None] == jnp.arange(group_cap, dtype=jnp.float32)
    ).astype(jnp.float32)
    expert_rank = jnp.where(named_expert > 0, before, -1.0).reshape(
        block_rows, group_count, local_count
    )
    slot_info = (
        jnp.einsum("rgc,rgl->gcl", group_place, expert_rank + 1.0, precision=lax.Precision.HIGHEST)
        - 1.0
    )
    placement = jnp.sum(slot_hit, axis=1).astype(jnp.bfloat16)
    outgoing = jnp.einsum("rs,rd->sd", placement, normed, preferred_element_type=jnp.float32)
    outgoing = outgoing.astype(jnp.bfloat16).reshape(
        group_count, local_count, expert_cap, lane_width
    )
    arrived = lax.all_to_all(
        lax.all_to_all(outgoing, "grp", split_axis=0, concat_axis=0, tiled=True),
        "loc",
        split_axis=1,
        concat_axis=1,
        tiled=True,
    )
    slot_rows = arrived.reshape(slot_count, lane_width)
    gate_part = jnp.dot(slot_rows, w_gate[0], preferred_element_type=jnp.float32)
    up_part = jnp.dot(slot_rows, w_up[0], preferred_element_type=jnp.float32)
    gate_pre, up_pre = (
        lax.psum(gate_part.astype(jnp.bfloat16), "tp").astype(jnp.float32),
        lax.psum(up_part.astype(jnp.bfloat16), "tp").astype(jnp.float32),
    )
    active = (jax.nn.silu(gate_pre) * up_pre).astype(jnp.bfloat16)
    expert_out = jnp.dot(active, w_down[0], preferred_element_type=jnp.float32).astype(jnp.bfloat16)
    out_blocks = expert_out.reshape(group_count, local_count, expert_cap, lane_width)
    slot_weight = jnp.einsum(
        "rgc,rgl->gcl",
        group_place,
        expert_weight.reshape(block_rows, group_count, local_count),
        precision=lax.Precision.HIGHEST,
    )
    rank_there, weight_there = (
        lax.all_to_all(slot_info, "grp", split_axis=0, concat_axis=0, tiled=True),
        lax.all_to_all(slot_weight, "grp", split_axis=0, concat_axis=0, tiled=True),
    )
    at_group = lax.all_to_all(out_blocks, "loc", split_axis=1, concat_axis=1, tiled=True)
    picks = (rank_there[:, :, :, None] == jnp.arange(expert_cap, dtype=jnp.float32)).astype(
        jnp.float32
    )
    picks = picks * weight_there[:, :, :, None]
    summed = jnp.einsum(
        "gclp,glpd->gcd", picks, at_group.astype(jnp.float32), precision=lax.Precision.HIGHEST
    ).astype(jnp.bfloat16)
    at_owner = lax.all_to_all(summed, "grp", split_axis=0, concat_axis=0, tiled=True)
    layer_out = mixed + jnp.einsum(
        "rgc,gcd->rd", group_place, at_owner.astype(jnp.float32), precision=lax.Precision.HIGHEST
    )
    return layer_out.astype(jnp.bfloat16)


def dense_kernel(
    sizes, resid_hbm, heads, proj, gain_hbm, ids_hbm, scores_hbm, w_gate, w_up, w_down, out,
    resid, gain, ids, scores, heads_v, proj_v, gate_v, up_v, down_v, rs_out, rs_in, mixed, rows, sq_out, sq_in, info,
    core_out, core_in, own, y_out, y_in, active, kept_down, pair_out, pair_in, part_out, part_in,
    local_sem, send_sem, recv_sem,
):
    groups, tp_count, parts, out_parts = sizes
    block, width = resid.shape
    depth = heads.shape[1]
    ff = gate_v.shape[1]
    piece = width // parts
    out_piece = width // out_parts
    fpiece = ff // tp_count
    tall = groups * block
    g, l, t = lax.axis_index("grp"), lax.axis_index("loc"), lax.axis_index("tp")
    core, y = lax.rem(t, 2), t // 2
    core_peer = t + 1 - 2 * core
    y_peer = t + 2 - 4 * y
    diagonal = core_peer + 2 - 4 * y
    at_core, at_y, at_x = {"tp": core_peer}, {"tp": y_peer}, {"loc": 1 - l}

    def at_group(step):
        return {"grp": lax.rem(g + step + groups, groups)}

    barrier = pltpu.get_barrier_semaphore()
    friends = [{"tp": lax.rem(t + r, tp_count)} for r in range(1, tp_count)]
    friends += [at_group(d) for d in range(1, groups)]
    friends += [{**at_group(d), **at_x} for d in range(groups)]
    for friend in friends:
        pl.semaphore_signal(barrier, inc=1, device_id=friend, device_id_type=MESH)

    local_count = [0]

    def fetch(src, dst):
        copy = pltpu.make_async_copy(src, dst, local_sem.at[local_count[0]])
        local_count[0] += 1
        return copy

    started = []
    remote_count = [0]

    def send(src, dst, device):
        n = remote_count[0]
        remote_count[0] += 1
        copy = pltpu.make_async_remote_copy(
            src_ref=src, dst_ref=dst, send_sem=send_sem.at[n], recv_sem=recv_sem.at[n],
            device_id=device, device_id_type=MESH,
        )
        copy.start()
        started.append(copy)
        return copy

    get_heads = fetch(heads, heads_v)
    half = depth // 2
    get_proj = [
        fetch(
            proj.at[pl.ds(k * half, half), pl.ds(c * piece, piece)],
            proj_v.at[c, pl.ds(k * half, half)],
        )
        for c in range(parts)
        for k in range(2)
    ]
    get_small = [
        fetch(ids_hbm, ids), fetch(scores_hbm, scores), fetch(gain_hbm, gain),
        fetch(resid_hbm, resid),
    ]
    get_gate = fetch(w_gate.at[0], gate_v)
    get_up = fetch(w_up.at[0], up_v)
    get_down = fetch(w_down.at[0], down_v)
    queue = get_proj + [get_gate, get_up, get_down]
    for copy in [get_heads] + queue[:2] + get_small + queue[2:3]:
        copy.start()
    for copy in get_small:
        copy.wait()

    lane = lax.broadcasted_iota(jnp.int32, (block, LANES), 1)
    square_row = lax.broadcasted_iota(jnp.int32, (block, block), 0)
    square_lane = lax.broadcasted_iota(jnp.int32, (block, block), 1)
    expert_count = ids.shape[0]

    def upright(row):
        return jnp.sum(jnp.where(square_row == square_lane, row, 0.0), axis=1, keepdims=True)

    score = scores[...].astype(jnp.float32)
    score = route_scale * score / jnp.sum(score, axis=0, keepdims=True)
    named = ids[...].astype(jnp.float32)
    weights = jnp.zeros((block, LANES), jnp.float32)
    for k in range(expert_count):
        column = upright(named[k : k + 1]).astype(jnp.int32)
        weights += jnp.where(column == lane, upright(score[k : k + 1]), 0.0)

    rs, spread, forward = {}, {}, {}
    keep = [None] * parts
    square = [jnp.zeros((block, 1), jnp.float32)]

    def settle(c):
        columns = pl.ds(c * piece, piece)
        rs[c].wait_recv()
        total = resid[:, columns].astype(jnp.float32) + (keep[c] + rs_in[c].astype(jnp.float32))
        mixed[:, columns] = total
        square[0] += jnp.sum(total * total, axis=1, keepdims=True)
        rows[0, 0, :, columns] = (total * gain[:, columns]).astype(jnp.bfloat16)
        mine = rows.at[0, 0, :, columns]
        forward[c, 0] = send(mine, rows.at[1, 0, :, columns], at_x)
        for d in range(groups - 1, 0, -1):
            spread[c, d] = send(mine, rows.at[0, d, :, columns], at_group(d))

    def pass_on(c):
        columns = pl.ds(c * piece, piece)
        for d in range(1, groups):
            spread[c, d].wait_recv()
            here = rows.at[0, d, :, columns]
            forward[c, d] = send(here, rows.at[1, d, :, columns], at_x)

    for c in range(parts):
        share = None
        for k in range(2):
            n = 2 * c + k
            queue[n].wait()
            if n + 3 < len(queue):
                queue[n + 3].start()
            if n == 0:
                get_heads.wait()
            term = jnp.dot(
                heads_v[:, pl.ds(k * half, half)],
                proj_v[c, pl.ds(k * half, half)],
                preferred_element_type=jnp.float32,
            )
            share = term if share is None else share + term
        low, high = share[:block], share[block:]
        keep[c] = jnp.where(l == 0, low, high)
        rs_out[c] = jnp.where(l == 0, high, low).astype(jnp.bfloat16)
        if c == 0:
            pl.semaphore_wait(barrier, len(friends))
        rs[c] = send(rs_out.at[c], rs_in.at[c], at_x)
        if c >= 1:
            settle(c - 1)
    early = max(parts - 2, 0)
    for c in range(early):
        pass_on(c)
    settle(parts - 1)

    sq_out[...] = jnp.broadcast_to(square[0], sq_out.shape)
    sums = [
        send(sq_out, sq_in.at[r - 1], {"tp": lax.rem(t + r, tp_count)})
        for r in range(1, tp_count)
    ]
    for c in range(early, parts):
        pass_on(c)

    told = {}

    def tell():
        total_square = sq_out[...]
        for r, copy in enumerate(sums):
            copy.wait_recv()
            total_square += sq_in[r]
        inverse = lax.rsqrt(total_square / (width * tp_count) + norm_eps)
        info[0, 0] = jnp.where(lane < expert_count, weights, inverse)
        for d in range(groups):
            told[1, d] = send(info.at[0, 0], info.at[1, d], {**at_group(d), **at_x})
        for d in range(1, groups):
            told[0, d] = send(info.at[0, 0], info.at[0, d], at_group(d))

    get_gate.wait()
    get_up.wait()

    def pair(side, q):
        x = rows[side].reshape(tall, width)
        columns = pl.ds(pl.multiple_of(q * fpiece, fpiece), fpiece)
        return (
            jnp.dot(x, gate_v[:, columns], preferred_element_type=jnp.float32),
            jnp.dot(x, up_v[:, columns], preferred_element_type=jnp.float32),
        )

    over_core, over_y, from_y, from_core, relay = {}, {}, {}, {}, {}

    def give(side):
        if side == 1:
            for c in range(parts):
                for d in range(groups):
                    forward[c, d].wait_recv()
        for n, q in enumerate((diagonal, core_peer)):
            for m, value in enumerate(pair(side, q)):
                core_out[side, n, m] = value.astype(jnp.bfloat16)
            over_core[side, n] = send(core_out.at[side, n], core_in.at[side, n], at_core)

    def hold(side):
        for n, q in enumerate((y_peer, t)):
            for m, value in enumerate(pair(side, q)):
                own[side, n, m] = value

    def cross(side):
        over_core[side, 0].wait_recv()
        y_out[side] = (own[side, 0] + core_in[side, 0].astype(jnp.float32)).astype(jnp.bfloat16)
        over_y[side] = send(y_out.at[side], y_in.at[side], at_y)

    def activate(side):
        over_core[side, 1].wait_recv()
        kept = own[side, 1] + core_in[side, 1].astype(jnp.float32)
        for d in range(groups):
            if (side, d) in told:
                told[side, d].wait_recv()
        known = info[side].reshape(tall, LANES)
        known_lane = lax.broadcasted_iota(jnp.int32, (tall, LANES), 1)
        expert = g * 2 + l
        scale = known[:, expert_count : expert_count + 1]
        weight = jnp.sum(jnp.where(known_lane == expert, known, 0.0), axis=1, keepdims=True)
        over_y[side].wait_recv()
        pre = (kept + y_in[side].astype(jnp.float32)) * scale
        gate_pre, up_pre = pre[0], pre[1]
        value = gate_pre / (1.0 + jnp.exp(-gate_pre)) * up_pre * weight
        active[side, 0] = value.astype(jnp.bfloat16)
        from_y[side] = send(active.at[side, 0], active.at[side, 2], at_y)
        from_core[side] = send(active.at[side, 0], active.at[side, 1], at_core)

    def hand_over(side):
        from_y[side].wait_recv()
        relay[side] = send(active.at[side, 2], active.at[side, 3], at_core)

    places = (t, core_peer, y_peer, diagonal)

    def down(side, c, first, last):
        columns = pl.ds(c * out_piece, out_piece)
        total = None
        for n in range(first, last):
            part = jnp.dot(
                active[side, n],
                down_v[pl.ds(pl.multiple_of(places[n] * fpiece, fpiece), fpiece), columns],
                preferred_element_type=jnp.float32,
            )
            total = part if total is None else total + part
        return total

    give(0)
    tell()
    hold(0)
    cross(0)
    give(1)
    hold(1)
    cross(1)
    get_down.wait()
    activate(0)
    activate(1)
    hand_over(0)
    from_core[0].wait_recv()
    for c in range(out_parts):
        kept_down[0, c] = down(0, c, 0, 3)
    hand_over(1)
    from_core[1].wait_recv()
    for c in range(out_parts):
        kept_down[1, c] = down(1, c, 0, 3)
    relay[1].wait_recv()
    across, home = {}, {}
    sent = len(started)
    for c in range(out_parts):
        pair_out[c] = (kept_down[1, c] + down(1, c, 3, 4)).astype(jnp.bfloat16)
        across[c] = send(pair_out.at[c], pair_in.at[c], at_x)
    relay[0].wait_recv()
    for c in range(out_parts):
        kept_down[0, c] += down(0, c, 3, 4)
    for copy in started[:sent]:
        copy.wait_send()
    for c in range(out_parts):
        across[c].wait_recv()
        summed = kept_down[0, c] + pair_in[c].astype(jnp.float32)
        part_out[c] = summed.astype(jnp.bfloat16).reshape(groups, block, out_piece)
        for d in range(1, groups):
            home[c, d] = send(part_out.at[c, d], part_in.at[c, d - 1], at_group(-d))
    for c in range(out_parts):
        columns = pl.ds(c * out_piece, out_piece)
        total = mixed[:, columns] + part_out[c, 0].astype(jnp.float32)
        for d in range(1, groups):
            home[c, d].wait_recv()
            total += part_in[c, d - 1].astype(jnp.float32)
        out[:, columns] = total.astype(out.dtype)
    for copy in started[sent:]:
        copy.wait_send()


def dense(resid_in, attn_heads, out_proj, norm_gain, expert_ids, gate_scores, w_gate, w_up, w_down):
    groups, tp_count = lax.axis_size("grp"), lax.axis_size("tp")
    block, width = resid_in.shape
    heads_shape = attn_heads.shape
    ff = w_gate.shape[2]
    fpiece = ff // tp_count
    tall = groups * block
    parts, out_parts = 4, 4
    piece, out_piece = width // parts, width // out_parts
    bf16, f32 = jnp.bfloat16, jnp.float32
    local_copies = 8 + 2 * parts
    remote_copies = (
        parts + parts * (2 * groups - 1) + (tp_count - 1) + (2 * groups - 1) + 4 + 2 + 6
        + out_parts * groups
    )
    vmem = pl.BlockSpec(memory_space=pltpu.VMEM)
    return pl.pallas_call(
        functools.partial(dense_kernel, (groups, tp_count, parts, out_parts)),
        out_shape=jax.ShapeDtypeStruct(resid_in.shape, bf16),
        in_specs=[pl.BlockSpec(memory_space=pltpu.HBM)] * 9,
        out_specs=vmem,
        scratch_shapes=[
            pltpu.VMEM((block, width), bf16),
            pltpu.VMEM((1, width), f32),
            pltpu.VMEM(expert_ids.shape[::-1], jnp.int32),
            pltpu.VMEM(gate_scores.shape[::-1], jnp.int32),
            pltpu.VMEM(heads_shape, bf16),
            pltpu.VMEM((parts, heads_shape[1], piece), bf16),
            pltpu.VMEM((width, ff), bf16),
            pltpu.VMEM((width, ff), bf16),
            pltpu.VMEM((ff, width), bf16),
            pltpu.VMEM((parts, block, piece), bf16),
            pltpu.VMEM((parts, block, piece), bf16),
            pltpu.VMEM((block, width), f32),
            pltpu.VMEM((2, groups, block, width), bf16),
            pltpu.VMEM((block, LANES), f32),
            pltpu.VMEM((tp_count - 1, block, LANES), f32),
            pltpu.VMEM((2, groups, block, LANES), f32),
            pltpu.VMEM((2, 2, 2, tall, fpiece), bf16),
            pltpu.VMEM((2, 2, 2, tall, fpiece), bf16),
            pltpu.VMEM((2, 2, 2, tall, fpiece), f32),
            pltpu.VMEM((2, 2, tall, fpiece), bf16),
            pltpu.VMEM((2, 2, tall, fpiece), bf16),
            pltpu.VMEM((2, 4, tall, fpiece), bf16),
            pltpu.VMEM((2, out_parts, tall, out_piece), f32),
            pltpu.VMEM((out_parts, tall, out_piece), bf16),
            pltpu.VMEM((out_parts, tall, out_piece), bf16),
            pltpu.VMEM((out_parts, groups, block, out_piece), bf16),
            pltpu.VMEM((out_parts, groups - 1, block, out_piece), bf16),
            pltpu.SemaphoreType.DMA((local_copies,)),
            pltpu.SemaphoreType.DMA((remote_copies,)),
            pltpu.SemaphoreType.DMA((remote_copies,)),
        ],
        compiler_params=pltpu.CompilerParams(
            collective_id=0, has_side_effects=True, vmem_limit_bytes=64 * 1024 * 1024
        ),
    )(
        resid_in, attn_heads, out_proj, norm_gain.reshape(1, width), expert_ids.T, gate_scores.T,
        w_gate, w_up, w_down,
    )


def local(*arrays):
    expert_ids = arrays[4]
    expert_total = lax.axis_size("grp") * lax.axis_size("loc")
    if (
        expert_ids.shape[1] == expert_total
        and lax.axis_size("loc") == 2
        and lax.axis_size("tp") == 4
    ):
        return dense(*arrays)
    return routed(*arrays)


def solution(mesh):
    placed = (
        P(("grp", "loc"), "tp"),
        P("grp", "loc"),
        P("loc", "tp"),
        P("tp"),
        P(("grp", "loc"), None),
        P(("grp", "loc"), None),
        P(("grp", "loc"), "tp", None),
        P(("grp", "loc"), "tp", None),
        P(("grp", "loc"), None, "tp"),
    )
    return jax.shard_map(
        local, mesh=mesh, in_specs=placed, out_specs=P(("grp", "loc"), "tp"), check_vma=False
    )
```

```python
import functools

import jax
import jax.numpy as jnp
from jax import lax
from jax.experimental import pallas as pl
from jax.experimental.pallas import tpu as pltpu
from jax.sharding import PartitionSpec as P

MESH = pl.DeviceIdType.MESH
LANES = 128

D = 4096
KEEP = 4
PER = 2


route_scale = 2.5
norm_eps = 1e-06


def routed(resid_in, attn_heads, out_proj, norm_gain, expert_ids, gate_scores, w_gate, w_up, w_down):
    group_count = lax.axis_size("grp")
    local_count = lax.axis_size("loc")
    block_rows = resid_in.shape[0]
    lane_width = resid_in.shape[1]
    expert_total = group_count * local_count
    spread = group_count // KEEP
    group_cap = min(block_rows, 2 * block_rows // spread)
    expert_cap = PER * group_cap // local_count
    slot_count = expert_total * expert_cap
    attn_out = lax.psum_scatter(
        jnp.dot(attn_heads, out_proj, preferred_element_type=jnp.float32).astype(jnp.bfloat16),
        "loc",
        scatter_dimension=0,
        tiled=True,
    ).astype(jnp.float32)
    mixed = resid_in.astype(jnp.float32) + attn_out
    square_sum = lax.psum(jnp.sum(mixed * mixed, axis=1), "tp")
    inverse_rms = lax.rsqrt(square_sum / D + norm_eps)
    normed = (mixed * inverse_rms[:, None] * norm_gain).astype(jnp.bfloat16)
    scores = gate_scores.astype(jnp.float32)
    route_weight = route_scale * scores / jnp.sum(scores, axis=1, keepdims=True)
    expert_hit = (expert_ids[:, :, None] == jnp.arange(expert_total, dtype=jnp.int32)).astype(
        jnp.float32
    )
    named_expert = jnp.sum(expert_hit, axis=1)
    expert_weight = jnp.sum(expert_hit * route_weight[:, :, None], axis=1)
    earlier = (jnp.arange(block_rows)[:, None] > jnp.arange(block_rows)[None, :]).astype(
        jnp.float32
    )
    before = jnp.dot(earlier, named_expert, precision=lax.Precision.HIGHEST)
    position = jnp.sum(expert_hit * before[:, None, :], axis=2).astype(jnp.int32)
    slot_index = expert_ids * expert_cap + position
    slot_hit = (slot_index[:, :, None] == jnp.arange(slot_count, dtype=jnp.int32)).astype(
        jnp.float32
    )
    group_ids = expert_ids // local_count
    group_hit = (group_ids[:, :, None] == jnp.arange(group_count, dtype=jnp.int32)).astype(
        jnp.float32
    )
    group_named = jnp.minimum(jnp.sum(group_hit, axis=1), 1.0)
    group_before = jnp.dot(earlier, group_named, precision=lax.Precision.HIGHEST)
    group_place = group_named[:, :, None] * (
        group_before[:, :, None] == jnp.arange(group_cap, dtype=jnp.float32)
    ).astype(jnp.float32)
    expert_rank = jnp.where(named_expert > 0, before, -1.0).reshape(
        block_rows, group_count, local_count
    )
    slot_info = (
        jnp.einsum("rgc,rgl->gcl", group_place, expert_rank + 1.0, precision=lax.Precision.HIGHEST)
        - 1.0
    )
    placement = jnp.sum(slot_hit, axis=1).astype(jnp.bfloat16)
    outgoing = jnp.einsum("rs,rd->sd", placement, normed, preferred_element_type=jnp.float32)
    outgoing = outgoing.astype(jnp.bfloat16).reshape(
        group_count, local_count, expert_cap, lane_width
    )
    arrived = lax.all_to_all(
        lax.all_to_all(outgoing, "grp", split_axis=0, concat_axis=0, tiled=True),
        "loc",
        split_axis=1,
        concat_axis=1,
        tiled=True,
    )
    slot_rows = arrived.reshape(slot_count, lane_width)
    gate_part = jnp.dot(slot_rows, w_gate[0], preferred_element_type=jnp.float32)
    up_part = jnp.dot(slot_rows, w_up[0], preferred_element_type=jnp.float32)
    gate_pre, up_pre = (
        lax.psum(gate_part.astype(jnp.bfloat16), "tp").astype(jnp.float32),
        lax.psum(up_part.astype(jnp.bfloat16), "tp").astype(jnp.float32),
    )
    active = (jax.nn.silu(gate_pre) * up_pre).astype(jnp.bfloat16)
    expert_out = jnp.dot(active, w_down[0], preferred_element_type=jnp.float32).astype(jnp.bfloat16)
    out_blocks = expert_out.reshape(group_count, local_count, expert_cap, lane_width)
    slot_weight = jnp.einsum(
        "rgc,rgl->gcl",
        group_place,
        expert_weight.reshape(block_rows, group_count, local_count),
        precision=lax.Precision.HIGHEST,
    )
    rank_there, weight_there = (
        lax.all_to_all(slot_info, "grp", split_axis=0, concat_axis=0, tiled=True),
        lax.all_to_all(slot_weight, "grp", split_axis=0, concat_axis=0, tiled=True),
    )
    at_group = lax.all_to_all(out_blocks, "loc", split_axis=1, concat_axis=1, tiled=True)
    picks = (rank_there[:, :, :, None] == jnp.arange(expert_cap, dtype=jnp.float32)).astype(
        jnp.float32
    )
    picks = picks * weight_there[:, :, :, None]
    summed = jnp.einsum(
        "gclp,glpd->gcd", picks, at_group.astype(jnp.float32), precision=lax.Precision.HIGHEST
    ).astype(jnp.bfloat16)
    at_owner = lax.all_to_all(summed, "grp", split_axis=0, concat_axis=0, tiled=True)
    layer_out = mixed + jnp.einsum(
        "rgc,gcd->rd", group_place, at_owner.astype(jnp.float32), precision=lax.Precision.HIGHEST
    )
    return layer_out.astype(jnp.bfloat16)


def dense_kernel(
    sizes, resid_hbm, heads, proj, gain_hbm, ids_hbm, scores_hbm, w_gate, w_up, w_down, out,
    resid, gain, ids, scores, heads_v, proj_v, gate_v, up_v, down_v, rs_out, rs_in, mixed, rows, sq_out, sq_in, info,
    core_out, core_in, own, y_out, y_in, active, kept_down, pair_out, pair_in, part_out, part_in,
    local_sem, send_sem, recv_sem,
):
    groups, tp_count, parts, out_parts = sizes
    block, width = resid.shape
    depth = heads.shape[1]
    ff = gate_v.shape[1]
    piece = width // parts
    out_piece = width // out_parts
    fpiece = ff // tp_count
    tall = groups * block
    g, l, t = lax.axis_index("grp"), lax.axis_index("loc"), lax.axis_index("tp")
    core, y = lax.rem(t, 2), t // 2
    core_peer = t + 1 - 2 * core
    y_peer = t + 2 - 4 * y
    diagonal = core_peer + 2 - 4 * y
    at_core, at_y, at_x = {"tp": core_peer}, {"tp": y_peer}, {"loc": 1 - l}

    def at_group(step):
        return {"grp": lax.rem(g + step + groups, groups)}

    barrier = pltpu.get_barrier_semaphore()
    friends = [{"tp": lax.rem(t + r, tp_count)} for r in range(1, tp_count)]
    friends += [at_group(d) for d in range(1, groups)]
    friends += [{**at_group(d), **at_x} for d in range(groups)]
    for friend in friends:
        pl.semaphore_signal(barrier, inc=1, device_id=friend, device_id_type=MESH)

    local_count = [0]

    def fetch(src, dst):
        copy = pltpu.make_async_copy(src, dst, local_sem.at[local_count[0]])
        local_count[0] += 1
        return copy

    started = []
    remote_count = [0]

    def send(src, dst, device):
        n = remote_count[0]
        remote_count[0] += 1
        copy = pltpu.make_async_remote_copy(
            src_ref=src, dst_ref=dst, send_sem=send_sem.at[n], recv_sem=recv_sem.at[n],
            device_id=device, device_id_type=MESH,
        )
        copy.start()
        started.append(copy)
        return copy

    get_heads = fetch(heads, heads_v)
    splits = 8 // parts
    share_depth = depth // splits
    get_proj = [
        fetch(
            proj.at[pl.ds(k * share_depth, share_depth), pl.ds(c * piece, piece)],
            proj_v.at[c, pl.ds(k * share_depth, share_depth)],
        )
        for c in range(parts)
        for k in range(splits)
    ]
    get_small = [
        fetch(ids_hbm, ids), fetch(scores_hbm, scores), fetch(gain_hbm, gain),
        fetch(resid_hbm, resid),
    ]
    get_gate = fetch(w_gate.at[0], gate_v)
    get_up = fetch(w_up.at[0], up_v)
    get_down = fetch(w_down.at[0], down_v)
    queue = get_proj + [get_gate, get_up, get_down]
    for copy in [get_heads] + queue[:2] + get_small + queue[2:3]:
        copy.start()
    for copy in get_small:
        copy.wait()

    lane = lax.broadcasted_iota(jnp.int32, (block, LANES), 1)
    square_row = lax.broadcasted_iota(jnp.int32, (block, block), 0)
    square_lane = lax.broadcasted_iota(jnp.int32, (block, block), 1)
    expert_count = ids.shape[0]

    def upright(row):
        return jnp.sum(jnp.where(square_row == square_lane, row, 0.0), axis=1, keepdims=True)

    score = scores[...].astype(jnp.float32)
    score = route_scale * score / jnp.sum(score, axis=0, keepdims=True)
    named = ids[...].astype(jnp.float32)
    weights = jnp.zeros((block, LANES), jnp.float32)
    for k in range(expert_count):
        column = upright(named[k : k + 1]).astype(jnp.int32)
        weights += jnp.where(column == lane, upright(score[k : k + 1]), 0.0)

    rs, spread, forward = {}, {}, {}
    keep = [None] * parts
    square = [jnp.zeros((block, 1), jnp.float32)]

    def settle(c):
        columns = pl.ds(c * piece, piece)
        rs[c].wait_recv()
        total = resid[:, columns].astype(jnp.float32) + (keep[c] + rs_in[c].astype(jnp.float32))
        mixed[:, columns] = total
        square[0] += jnp.sum(total * total, axis=1, keepdims=True)
        rows[0, 0, :, columns] = (total * gain[:, columns]).astype(jnp.bfloat16)
        mine = rows.at[0, 0, :, columns]
        forward[c, 0] = send(mine, rows.at[1, 0, :, columns], at_x)
        for d in range(groups - 1, 0, -1):
            spread[c, d] = send(mine, rows.at[0, d, :, columns], at_group(d))

    def pass_on(c):
        columns = pl.ds(c * piece, piece)
        for d in range(1, groups):
            spread[c, d].wait_recv()
            here = rows.at[0, d, :, columns]
            forward[c, d] = send(here, rows.at[1, d, :, columns], at_x)

    for c in range(parts):
        share = None
        for k in range(splits):
            n = splits * c + k
            queue[n].wait()
            if n + 3 < len(queue):
                queue[n + 3].start()
            if n == 0:
                get_heads.wait()
            term = jnp.dot(
                heads_v[:, pl.ds(k * share_depth, share_depth)],
                proj_v[c, pl.ds(k * share_depth, share_depth)],
                preferred_element_type=jnp.float32,
            )
            share = term if share is None else share + term
        low, high = share[:block], share[block:]
        keep[c] = jnp.where(l == 0, low, high)
        rs_out[c] = jnp.where(l == 0, high, low).astype(jnp.bfloat16)
        if c == 0:
            pl.semaphore_wait(barrier, len(friends))
        rs[c] = send(rs_out.at[c], rs_in.at[c], at_x)
        if c >= 1:
            settle(c - 1)
    early = max(parts - 2, 0)
    for c in range(early):
        pass_on(c)
    settle(parts - 1)

    sq_out[...] = jnp.broadcast_to(square[0], sq_out.shape)
    sums = [
        send(sq_out, sq_in.at[r - 1], {"tp": lax.rem(t + r, tp_count)})
        for r in range(1, tp_count)
    ]
    for c in range(early, parts):
        pass_on(c)

    told = {}

    def tell():
        total_square = sq_out[...]
        for r, copy in enumerate(sums):
            copy.wait_recv()
            total_square += sq_in[r]
        inverse = lax.rsqrt(total_square / (width * tp_count) + norm_eps)
        info[0, 0] = jnp.where(lane < expert_count, weights, inverse)
        for d in range(groups):
            told[1, d] = send(info.at[0, 0], info.at[1, d], {**at_group(d), **at_x})
        for d in range(1, groups):
            told[0, d] = send(info.at[0, 0], info.at[0, d], at_group(d))

    get_gate.wait()
    get_up.wait()

    def pair(side, q):
        x = rows[side].reshape(tall, width)
        columns = pl.ds(pl.multiple_of(q * fpiece, fpiece), fpiece)
        return (
            jnp.dot(x, gate_v[:, columns], preferred_element_type=jnp.float32),
            jnp.dot(x, up_v[:, columns], preferred_element_type=jnp.float32),
        )

    over_core, over_y, from_y, from_core, relay = {}, {}, {}, {}, {}

    def give(side):
        if side == 1:
            for c in range(parts):
                for d in range(groups):
                    forward[c, d].wait_recv()
        for n, q in enumerate((diagonal, core_peer)):
            for m, value in enumerate(pair(side, q)):
                core_out[side, n, m] = value.astype(jnp.bfloat16)
            over_core[side, n] = send(core_out.at[side, n], core_in.at[side, n], at_core)

    def hold(side):
        for n, q in enumerate((y_peer, t)):
            for m, value in enumerate(pair(side, q)):
                own[side, n, m] = value

    def cross(side):
        over_core[side, 0].wait_recv()
        y_out[side] = (own[side, 0] + core_in[side, 0].astype(jnp.float32)).astype(jnp.bfloat16)
        over_y[side] = send(y_out.at[side], y_in.at[side], at_y)

    def activate(side):
        over_core[side, 1].wait_recv()
        kept = own[side, 1] + core_in[side, 1].astype(jnp.float32)
        for d in range(groups):
            if (side, d) in told:
                told[side, d].wait_recv()
        known = info[side].reshape(tall, LANES)
        known_lane = lax.broadcasted_iota(jnp.int32, (tall, LANES), 1)
        expert = g * 2 + l
        scale = known[:, expert_count : expert_count + 1]
        weight = jnp.sum(jnp.where(known_lane == expert, known, 0.0), axis=1, keepdims=True)
        over_y[side].wait_recv()
        pre = (kept + y_in[side].astype(jnp.float32)) * scale
        gate_pre, up_pre = pre[0], pre[1]
        value = gate_pre / (1.0 + jnp.exp(-gate_pre)) * up_pre * weight
        active[side, 0] = value.astype(jnp.bfloat16)
        from_y[side] = send(active.at[side, 0], active.at[side, 2], at_y)
        from_core[side] = send(active.at[side, 0], active.at[side, 1], at_core)

    def hand_over(side):
        from_y[side].wait_recv()
        relay[side] = send(active.at[side, 2], active.at[side, 3], at_core)

    places = (t, core_peer, y_peer, diagonal)

    def down(side, c, first, last):
        columns = pl.ds(c * out_piece, out_piece)
        total = None
        for n in range(first, last):
            part = jnp.dot(
                active[side, n],
                down_v[pl.ds(pl.multiple_of(places[n] * fpiece, fpiece), fpiece), columns],
                preferred_element_type=jnp.float32,
            )
            total = part if total is None else total + part
        return total

    give(0)
    tell()
    hold(0)
    cross(0)
    give(1)
    hold(1)
    cross(1)
    get_down.wait()
    activate(0)
    activate(1)
    hand_over(0)
    from_core[0].wait_recv()
    for c in range(out_parts):
        kept_down[0, c] = down(0, c, 0, 3)
    hand_over(1)
    from_core[1].wait_recv()
    for c in range(out_parts):
        kept_down[1, c] = down(1, c, 0, 3)
    relay[1].wait_recv()
    across, home = {}, {}
    sent = len(started)
    for c in range(out_parts):
        pair_out[c] = (kept_down[1, c] + down(1, c, 3, 4)).astype(jnp.bfloat16)
        across[c] = send(pair_out.at[c], pair_in.at[c], at_x)
    relay[0].wait_recv()
    for c in range(out_parts):
        kept_down[0, c] += down(0, c, 3, 4)
    for copy in started[:sent]:
        copy.wait_send()
    for c in range(out_parts):
        across[c].wait_recv()
        summed = kept_down[0, c] + pair_in[c].astype(jnp.float32)
        part_out[c] = summed.astype(jnp.bfloat16).reshape(groups, block, out_piece)
        for d in range(1, groups):
            home[c, d] = send(part_out.at[c, d], part_in.at[c, d - 1], at_group(-d))
    for c in range(out_parts):
        columns = pl.ds(c * out_piece, out_piece)
        total = mixed[:, columns] + part_out[c, 0].astype(jnp.float32)
        for d in range(1, groups):
            home[c, d].wait_recv()
            total += part_in[c, d - 1].astype(jnp.float32)
        out[:, columns] = total.astype(out.dtype)
    for copy in started[sent:]:
        copy.wait_send()


def dense(resid_in, attn_heads, out_proj, norm_gain, expert_ids, gate_scores, w_gate, w_up, w_down):
    groups, tp_count = lax.axis_size("grp"), lax.axis_size("tp")
    block, width = resid_in.shape
    heads_shape = attn_heads.shape
    ff = w_gate.shape[2]
    fpiece = ff // tp_count
    tall = groups * block
    parts, out_parts = 2, 2
    piece, out_piece = width // parts, width // out_parts
    bf16, f32 = jnp.bfloat16, jnp.float32
    local_copies = 16
    remote_copies = (
        parts + parts * (2 * groups - 1) + (tp_count - 1) + (2 * groups - 1) + 4 + 2 + 6
        + out_parts * groups
    )
    vmem = pl.BlockSpec(memory_space=pltpu.VMEM)
    return pl.pallas_call(
        functools.partial(dense_kernel, (groups, tp_count, parts, out_parts)),
        out_shape=jax.ShapeDtypeStruct(resid_in.shape, bf16),
        in_specs=[pl.BlockSpec(memory_space=pltpu.HBM)] * 9,
        out_specs=vmem,
        scratch_shapes=[
            pltpu.VMEM((block, width), bf16),
            pltpu.VMEM((1, width), f32),
            pltpu.VMEM(expert_ids.shape[::-1], jnp.int32),
            pltpu.VMEM(gate_scores.shape[::-1], jnp.int32),
            pltpu.VMEM(heads_shape, bf16),
            pltpu.VMEM((parts, heads_shape[1], piece), bf16),
            pltpu.VMEM((width, ff), bf16),
            pltpu.VMEM((width, ff), bf16),
            pltpu.VMEM((ff, width), bf16),
            pltpu.VMEM((parts, block, piece), bf16),
            pltpu.VMEM((parts, block, piece), bf16),
            pltpu.VMEM((block, width), f32),
            pltpu.VMEM((2, groups, block, width), bf16),
            pltpu.VMEM((block, LANES), f32),
            pltpu.VMEM((tp_count - 1, block, LANES), f32),
            pltpu.VMEM((2, groups, block, LANES), f32),
            pltpu.VMEM((2, 2, 2, tall, fpiece), bf16),
            pltpu.VMEM((2, 2, 2, tall, fpiece), bf16),
            pltpu.VMEM((2, 2, 2, tall, fpiece), f32),
            pltpu.VMEM((2, 2, tall, fpiece), bf16),
            pltpu.VMEM((2, 2, tall, fpiece), bf16),
            pltpu.VMEM((2, 4, tall, fpiece), bf16),
            pltpu.VMEM((2, out_parts, tall, out_piece), f32),
            pltpu.VMEM((out_parts, tall, out_piece), bf16),
            pltpu.VMEM((out_parts, tall, out_piece), bf16),
            pltpu.VMEM((out_parts, groups, block, out_piece), bf16),
            pltpu.VMEM((out_parts, groups - 1, block, out_piece), bf16),
            pltpu.SemaphoreType.DMA((local_copies,)),
            pltpu.SemaphoreType.DMA((remote_copies,)),
            pltpu.SemaphoreType.DMA((remote_copies,)),
        ],
        compiler_params=pltpu.CompilerParams(
            collective_id=0, has_side_effects=True, vmem_limit_bytes=64 * 1024 * 1024
        ),
    )(
        resid_in, attn_heads, out_proj, norm_gain.reshape(1, width), expert_ids.T, gate_scores.T,
        w_gate, w_up, w_down,
    )


def local(*arrays):
    expert_ids = arrays[4]
    expert_total = lax.axis_size("grp") * lax.axis_size("loc")
    if (
        expert_ids.shape[1] == expert_total
        and lax.axis_size("loc") == 2
        and lax.axis_size("tp") == 4
    ):
        return dense(*arrays)
    return routed(*arrays)


def solution(mesh):
    placed = (
        P(("grp", "loc"), "tp"),
        P("grp", "loc"),
        P("loc", "tp"),
        P("tp"),
        P(("grp", "loc"), None),
        P(("grp", "loc"), None),
        P(("grp", "loc"), "tp", None),
        P(("grp", "loc"), "tp", None),
        P(("grp", "loc"), None, "tp"),
    )
    return jax.shard_map(
        local, mesh=mesh, in_specs=placed, out_specs=P(("grp", "loc"), "tp"), check_vma=False
    )
```

```python
import functools

import jax
import jax.numpy as jnp
from jax import lax
from jax.experimental import pallas as pl
from jax.experimental.pallas import tpu as pltpu
from jax.sharding import PartitionSpec as P

MESH = pl.DeviceIdType.MESH
LANES = 128

D = 4096
KEEP = 4
PER = 2


route_scale = 2.5
norm_eps = 1e-06


def routed(resid_in, attn_heads, out_proj, norm_gain, expert_ids, gate_scores, w_gate, w_up, w_down):
    group_count = lax.axis_size("grp")
    local_count = lax.axis_size("loc")
    block_rows = resid_in.shape[0]
    lane_width = resid_in.shape[1]
    expert_total = group_count * local_count
    spread = group_count // KEEP
    group_cap = min(block_rows, 2 * block_rows // spread)
    expert_cap = PER * group_cap // local_count
    slot_count = expert_total * expert_cap
    attn_out = lax.psum_scatter(
        jnp.dot(attn_heads, out_proj, preferred_element_type=jnp.float32).astype(jnp.bfloat16),
        "loc",
        scatter_dimension=0,
        tiled=True,
    ).astype(jnp.float32)
    mixed = resid_in.astype(jnp.float32) + attn_out
    square_sum = lax.psum(jnp.sum(mixed * mixed, axis=1), "tp")
    inverse_rms = lax.rsqrt(square_sum / D + norm_eps)
    normed = (mixed * inverse_rms[:, None] * norm_gain).astype(jnp.bfloat16)
    scores = gate_scores.astype(jnp.float32)
    route_weight = route_scale * scores / jnp.sum(scores, axis=1, keepdims=True)
    expert_hit = (expert_ids[:, :, None] == jnp.arange(expert_total, dtype=jnp.int32)).astype(
        jnp.float32
    )
    named_expert = jnp.sum(expert_hit, axis=1)
    expert_weight = jnp.sum(expert_hit * route_weight[:, :, None], axis=1)
    earlier = (jnp.arange(block_rows)[:, None] > jnp.arange(block_rows)[None, :]).astype(
        jnp.float32
    )
    before = jnp.dot(earlier, named_expert, precision=lax.Precision.HIGHEST)
    position = jnp.sum(expert_hit * before[:, None, :], axis=2).astype(jnp.int32)
    slot_index = expert_ids * expert_cap + position
    slot_hit = (slot_index[:, :, None] == jnp.arange(slot_count, dtype=jnp.int32)).astype(
        jnp.float32
    )
    group_ids = expert_ids // local_count
    group_hit = (group_ids[:, :, None] == jnp.arange(group_count, dtype=jnp.int32)).astype(
        jnp.float32
    )
    group_named = jnp.minimum(jnp.sum(group_hit, axis=1), 1.0)
    group_before = jnp.dot(earlier, group_named, precision=lax.Precision.HIGHEST)
    group_place = group_named[:, :, None] * (
        group_before[:, :, None] == jnp.arange(group_cap, dtype=jnp.float32)
    ).astype(jnp.float32)
    expert_rank = jnp.where(named_expert > 0, before, -1.0).reshape(
        block_rows, group_count, local_count
    )
    slot_info = (
        jnp.einsum("rgc,rgl->gcl", group_place, expert_rank + 1.0, precision=lax.Precision.HIGHEST)
        - 1.0
    )
    placement = jnp.sum(slot_hit, axis=1).astype(jnp.bfloat16)
    outgoing = jnp.einsum("rs,rd->sd", placement, normed, preferred_element_type=jnp.float32)
    outgoing = outgoing.astype(jnp.bfloat16).reshape(
        group_count, local_count, expert_cap, lane_width
    )
    arrived = lax.all_to_all(
        lax.all_to_all(outgoing, "grp", split_axis=0, concat_axis=0, tiled=True),
        "loc",
        split_axis=1,
        concat_axis=1,
        tiled=True,
    )
    slot_rows = arrived.reshape(slot_count, lane_width)
    gate_part = jnp.dot(slot_rows, w_gate[0], preferred_element_type=jnp.float32)
    up_part = jnp.dot(slot_rows, w_up[0], preferred_element_type=jnp.float32)
    gate_pre, up_pre = (
        lax.psum(gate_part.astype(jnp.bfloat16), "tp").astype(jnp.float32),
        lax.psum(up_part.astype(jnp.bfloat16), "tp").astype(jnp.float32),
    )
    active = (jax.nn.silu(gate_pre) * up_pre).astype(jnp.bfloat16)
    expert_out = jnp.dot(active, w_down[0], preferred_element_type=jnp.float32).astype(jnp.bfloat16)
    out_blocks = expert_out.reshape(group_count, local_count, expert_cap, lane_width)
    slot_weight = jnp.einsum(
        "rgc,rgl->gcl",
        group_place,
        expert_weight.reshape(block_rows, group_count, local_count),
        precision=lax.Precision.HIGHEST,
    )
    rank_there, weight_there = (
        lax.all_to_all(slot_info, "grp", split_axis=0, concat_axis=0, tiled=True),
        lax.all_to_all(slot_weight, "grp", split_axis=0, concat_axis=0, tiled=True),
    )
    at_group = lax.all_to_all(out_blocks, "loc", split_axis=1, concat_axis=1, tiled=True)
    picks = (rank_there[:, :, :, None] == jnp.arange(expert_cap, dtype=jnp.float32)).astype(
        jnp.float32
    )
    picks = picks * weight_there[:, :, :, None]
    summed = jnp.einsum(
        "gclp,glpd->gcd", picks, at_group.astype(jnp.float32), precision=lax.Precision.HIGHEST
    ).astype(jnp.bfloat16)
    at_owner = lax.all_to_all(summed, "grp", split_axis=0, concat_axis=0, tiled=True)
    layer_out = mixed + jnp.einsum(
        "rgc,gcd->rd", group_place, at_owner.astype(jnp.float32), precision=lax.Precision.HIGHEST
    )
    return layer_out.astype(jnp.bfloat16)


def dense_kernel(
    sizes, resid_hbm, heads, proj, gain_hbm, ids_hbm, scores_hbm, w_gate, w_up, w_down, out,
    resid, gain, ids, scores, heads_v, proj_v, gate_v, up_v, down_v, rs_out, rs_in, mixed, rows, sq_out, sq_in, info,
    core_out, core_in, own, y_out, y_in, active, kept_down, pair_out, pair_in, part_out, part_in,
    local_sem, send_sem, recv_sem,
):
    groups, tp_count, parts, out_parts = sizes
    block, width = resid.shape
    depth = heads.shape[1]
    ff = gate_v.shape[1]
    piece = width // parts
    out_piece = width // out_parts
    fpiece = ff // tp_count
    tall = groups * block
    g, l, t = lax.axis_index("grp"), lax.axis_index("loc"), lax.axis_index("tp")
    core, y = lax.rem(t, 2), t // 2
    core_peer = t + 1 - 2 * core
    y_peer = t + 2 - 4 * y
    diagonal = core_peer + 2 - 4 * y
    at_core, at_y, at_x = {"tp": core_peer}, {"tp": y_peer}, {"loc": 1 - l}

    def at_group(step):
        return {"grp": lax.rem(g + step + groups, groups)}

    barrier = pltpu.get_barrier_semaphore()
    friends = [{"tp": lax.rem(t + r, tp_count)} for r in range(1, tp_count)]
    friends += [at_group(d) for d in range(1, groups)]
    friends += [{**at_group(d), **at_x} for d in range(groups)]
    for friend in friends:
        pl.semaphore_signal(barrier, inc=1, device_id=friend, device_id_type=MESH)

    local_count = [0]

    def fetch(src, dst):
        copy = pltpu.make_async_copy(src, dst, local_sem.at[local_count[0]])
        local_count[0] += 1
        return copy

    started = []
    remote_count = [0]

    def send(src, dst, device):
        n = remote_count[0]
        remote_count[0] += 1
        copy = pltpu.make_async_remote_copy(
            src_ref=src, dst_ref=dst, send_sem=send_sem.at[n], recv_sem=recv_sem.at[n],
            device_id=device, device_id_type=MESH,
        )
        copy.start()
        started.append(copy)
        return copy

    get_heads = fetch(heads, heads_v)
    splits = 8 // parts
    share_depth = depth // splits
    get_proj = [
        fetch(
            proj.at[pl.ds(k * share_depth, share_depth), pl.ds(c * piece, piece)],
            proj_v.at[c, pl.ds(k * share_depth, share_depth)],
        )
        for c in range(parts)
        for k in range(splits)
    ]
    get_small = [
        fetch(ids_hbm, ids), fetch(scores_hbm, scores), fetch(gain_hbm, gain),
        fetch(resid_hbm, resid),
    ]
    get_gate = fetch(w_gate.at[0], gate_v)
    get_up = fetch(w_up.at[0], up_v)
    get_down = fetch(w_down.at[0], down_v)
    queue = get_proj + [get_gate, get_up, get_down]
    for copy in [get_heads] + queue[:2] + get_small + queue[2:3]:
        copy.start()
    for copy in get_small:
        copy.wait()

    lane = lax.broadcasted_iota(jnp.int32, (block, LANES), 1)
    square_row = lax.broadcasted_iota(jnp.int32, (block, block), 0)
    square_lane = lax.broadcasted_iota(jnp.int32, (block, block), 1)
    expert_count = ids.shape[0]

    def upright(row):
        return jnp.sum(jnp.where(square_row == square_lane, row, 0.0), axis=1, keepdims=True)

    score = scores[...].astype(jnp.float32)
    score = route_scale * score / jnp.sum(score, axis=0, keepdims=True)
    named = ids[...].astype(jnp.float32)
    weights = jnp.zeros((block, LANES), jnp.float32)
    for k in range(expert_count):
        column = upright(named[k : k + 1]).astype(jnp.int32)
        weights += jnp.where(column == lane, upright(score[k : k + 1]), 0.0)

    rs, spread, forward = {}, {}, {}
    keep = [None] * parts
    square = [jnp.zeros((block, 1), jnp.float32)]

    def settle(c):
        columns = pl.ds(c * piece, piece)
        rs[c].wait_recv()
        total = resid[:, columns].astype(jnp.float32) + (keep[c] + rs_in[c].astype(jnp.float32))
        mixed[:, columns] = total
        square[0] += jnp.sum(total * total, axis=1, keepdims=True)
        rows[0, 0, :, columns] = (total * gain[:, columns]).astype(jnp.bfloat16)
        mine = rows.at[0, 0, :, columns]
        forward[c, 0] = send(mine, rows.at[1, 0, :, columns], at_x)
        for d in range(groups - 1, 0, -1):
            spread[c, d] = send(mine, rows.at[0, d, :, columns], at_group(d))

    def pass_on(c):
        columns = pl.ds(c * piece, piece)
        for d in range(1, groups):
            spread[c, d].wait_recv()
            here = rows.at[0, d, :, columns]
            forward[c, d] = send(here, rows.at[1, d, :, columns], at_x)

    for c in range(parts):
        share = None
        for k in range(splits):
            n = splits * c + k
            queue[n].wait()
            if n + 3 < len(queue):
                queue[n + 3].start()
            if n == 0:
                get_heads.wait()
            term = jnp.dot(
                heads_v[:, pl.ds(k * share_depth, share_depth)],
                proj_v[c, pl.ds(k * share_depth, share_depth)],
                preferred_element_type=jnp.float32,
            )
            share = term if share is None else share + term
        low, high = share[:block], share[block:]
        keep[c] = jnp.where(l == 0, low, high)
        rs_out[c] = jnp.where(l == 0, high, low).astype(jnp.bfloat16)
        if c == 0:
            pl.semaphore_wait(barrier, len(friends))
        rs[c] = send(rs_out.at[c], rs_in.at[c], at_x)
        if c >= 1:
            settle(c - 1)
    early = max(parts - 2, 0)
    for c in range(early):
        pass_on(c)
    settle(parts - 1)

    sq_out[...] = jnp.broadcast_to(square[0], sq_out.shape)
    sums = [
        send(sq_out, sq_in.at[r - 1], {"tp": lax.rem(t + r, tp_count)})
        for r in range(1, tp_count)
    ]
    for c in range(early, parts):
        pass_on(c)

    told = {}

    def tell():
        total_square = sq_out[...]
        for r, copy in enumerate(sums):
            copy.wait_recv()
            total_square += sq_in[r]
        inverse = lax.rsqrt(total_square / (width * tp_count) + norm_eps)
        info[0, 0] = jnp.where(lane < expert_count, weights, inverse)
        for d in range(groups):
            told[1, d] = send(info.at[0, 0], info.at[1, d], {**at_group(d), **at_x})
        for d in range(1, groups):
            told[0, d] = send(info.at[0, 0], info.at[0, d], at_group(d))

    get_gate.wait()
    get_up.wait()

    def pair(side, q):
        x = rows[side].reshape(tall, width)
        columns = pl.ds(pl.multiple_of(q * fpiece, fpiece), fpiece)
        return (
            jnp.dot(x, gate_v[:, columns], preferred_element_type=jnp.float32),
            jnp.dot(x, up_v[:, columns], preferred_element_type=jnp.float32),
        )

    over_core, over_y, from_y, from_core, relay = {}, {}, {}, {}, {}

    def give(side):
        if side == 1:
            for c in range(parts):
                for d in range(groups):
                    forward[c, d].wait_recv()
        for n, q in enumerate((diagonal, core_peer)):
            for m, value in enumerate(pair(side, q)):
                core_out[side, n, m] = value.astype(jnp.bfloat16)
            over_core[side, n] = send(core_out.at[side, n], core_in.at[side, n], at_core)

    def hold(side):
        for n, q in enumerate((y_peer, t)):
            for m, value in enumerate(pair(side, q)):
                own[side, n, m] = value

    def cross(side):
        over_core[side, 0].wait_recv()
        y_out[side] = (own[side, 0] + core_in[side, 0].astype(jnp.float32)).astype(jnp.bfloat16)
        over_y[side] = send(y_out.at[side], y_in.at[side], at_y)

    def activate(side):
        over_core[side, 1].wait_recv()
        kept = own[side, 1] + core_in[side, 1].astype(jnp.float32)
        for d in range(groups):
            if (side, d) in told:
                told[side, d].wait_recv()
        known = info[side].reshape(tall, LANES)
        known_lane = lax.broadcasted_iota(jnp.int32, (tall, LANES), 1)
        expert = g * 2 + l
        scale = known[:, expert_count : expert_count + 1]
        weight = jnp.sum(jnp.where(known_lane == expert, known, 0.0), axis=1, keepdims=True)
        over_y[side].wait_recv()
        pre = (kept + y_in[side].astype(jnp.float32)) * scale
        gate_pre, up_pre = pre[0], pre[1]
        value = gate_pre / (1.0 + jnp.exp(-gate_pre)) * up_pre * weight
        active[side, 0] = value.astype(jnp.bfloat16)
        from_y[side] = send(active.at[side, 0], active.at[side, 2], at_y)
        from_core[side] = send(active.at[side, 0], active.at[side, 1], at_core)
        relay[side] = send(active.at[side, 0], active.at[side, 3], {"tp": diagonal})

    def hand_over(side):
        from_y[side].wait_recv()

    places = (t, core_peer, y_peer, diagonal)

    def down(side, c, first, last):
        columns = pl.ds(c * out_piece, out_piece)
        total = None
        for n in range(first, last):
            part = jnp.dot(
                active[side, n],
                down_v[pl.ds(pl.multiple_of(places[n] * fpiece, fpiece), fpiece), columns],
                preferred_element_type=jnp.float32,
            )
            total = part if total is None else total + part
        return total

    give(0)
    tell()
    hold(0)
    cross(0)
    give(1)
    hold(1)
    cross(1)
    get_down.wait()
    activate(0)
    activate(1)
    hand_over(0)
    from_core[0].wait_recv()
    for c in range(out_parts):
        kept_down[0, c] = down(0, c, 0, 3)
    hand_over(1)
    from_core[1].wait_recv()
    for c in range(out_parts):
        kept_down[1, c] = down(1, c, 0, 3)
    relay[1].wait_recv()
    across, home = {}, {}
    sent = len(started)
    for c in range(out_parts):
        pair_out[c] = (kept_down[1, c] + down(1, c, 3, 4)).astype(jnp.bfloat16)
        across[c] = send(pair_out.at[c], pair_in.at[c], at_x)
    relay[0].wait_recv()
    for c in range(out_parts):
        kept_down[0, c] += down(0, c, 3, 4)
    for copy in started[:sent]:
        copy.wait_send()
    for c in range(out_parts):
        across[c].wait_recv()
        summed = kept_down[0, c] + pair_in[c].astype(jnp.float32)
        part_out[c] = summed.astype(jnp.bfloat16).reshape(groups, block, out_piece)
        for d in range(1, groups):
            home[c, d] = send(part_out.at[c, d], part_in.at[c, d - 1], at_group(-d))
    for c in range(out_parts):
        columns = pl.ds(c * out_piece, out_piece)
        total = mixed[:, columns] + part_out[c, 0].astype(jnp.float32)
        for d in range(1, groups):
            home[c, d].wait_recv()
            total += part_in[c, d - 1].astype(jnp.float32)
        out[:, columns] = total.astype(out.dtype)
    for copy in started[sent:]:
        copy.wait_send()


def dense(resid_in, attn_heads, out_proj, norm_gain, expert_ids, gate_scores, w_gate, w_up, w_down):
    groups, tp_count = lax.axis_size("grp"), lax.axis_size("tp")
    block, width = resid_in.shape
    heads_shape = attn_heads.shape
    ff = w_gate.shape[2]
    fpiece = ff // tp_count
    tall = groups * block
    parts, out_parts = 2, 2
    piece, out_piece = width // parts, width // out_parts
    bf16, f32 = jnp.bfloat16, jnp.float32
    local_copies = 16
    remote_copies = (
        parts + parts * (2 * groups - 1) + (tp_count - 1) + (2 * groups - 1) + 4 + 2 + 6
        + out_parts * groups
    )
    vmem = pl.BlockSpec(memory_space=pltpu.VMEM)
    return pl.pallas_call(
        functools.partial(dense_kernel, (groups, tp_count, parts, out_parts)),
        out_shape=jax.ShapeDtypeStruct(resid_in.shape, bf16),
        in_specs=[pl.BlockSpec(memory_space=pltpu.HBM)] * 9,
        out_specs=vmem,
        scratch_shapes=[
            pltpu.VMEM((block, width), bf16),
            pltpu.VMEM((1, width), f32),
            pltpu.VMEM(expert_ids.shape[::-1], jnp.int32),
            pltpu.VMEM(gate_scores.shape[::-1], jnp.int32),
            pltpu.VMEM(heads_shape, bf16),
            pltpu.VMEM((parts, heads_shape[1], piece), bf16),
            pltpu.VMEM((width, ff), bf16),
            pltpu.VMEM((width, ff), bf16),
            pltpu.VMEM((ff, width), bf16),
            pltpu.VMEM((parts, block, piece), bf16),
            pltpu.VMEM((parts, block, piece), bf16),
            pltpu.VMEM((block, width), f32),
            pltpu.VMEM((2, groups, block, width), bf16),
            pltpu.VMEM((block, LANES), f32),
            pltpu.VMEM((tp_count - 1, block, LANES), f32),
            pltpu.VMEM((2, groups, block, LANES), f32),
            pltpu.VMEM((2, 2, 2, tall, fpiece), bf16),
            pltpu.VMEM((2, 2, 2, tall, fpiece), bf16),
            pltpu.VMEM((2, 2, 2, tall, fpiece), f32),
            pltpu.VMEM((2, 2, tall, fpiece), bf16),
            pltpu.VMEM((2, 2, tall, fpiece), bf16),
            pltpu.VMEM((2, 4, tall, fpiece), bf16),
            pltpu.VMEM((2, out_parts, tall, out_piece), f32),
            pltpu.VMEM((out_parts, tall, out_piece), bf16),
            pltpu.VMEM((out_parts, tall, out_piece), bf16),
            pltpu.VMEM((out_parts, groups, block, out_piece), bf16),
            pltpu.VMEM((out_parts, groups - 1, block, out_piece), bf16),
            pltpu.SemaphoreType.DMA((local_copies,)),
            pltpu.SemaphoreType.DMA((remote_copies,)),
            pltpu.SemaphoreType.DMA((remote_copies,)),
        ],
        compiler_params=pltpu.CompilerParams(
            collective_id=0, has_side_effects=True, vmem_limit_bytes=64 * 1024 * 1024
        ),
    )(
        resid_in, attn_heads, out_proj, norm_gain.reshape(1, width), expert_ids.T, gate_scores.T,
        w_gate, w_up, w_down,
    )


def local(*arrays):
    expert_ids = arrays[4]
    expert_total = lax.axis_size("grp") * lax.axis_size("loc")
    if (
        expert_ids.shape[1] == expert_total
        and lax.axis_size("loc") == 2
        and lax.axis_size("tp") == 4
    ):
        return dense(*arrays)
    return routed(*arrays)


def solution(mesh):
    placed = (
        P(("grp", "loc"), "tp"),
        P("grp", "loc"),
        P("loc", "tp"),
        P("tp"),
        P(("grp", "loc"), None),
        P(("grp", "loc"), None),
        P(("grp", "loc"), "tp", None),
        P(("grp", "loc"), "tp", None),
        P(("grp", "loc"), None, "tp"),
    )
    return jax.shard_map(
        local, mesh=mesh, in_specs=placed, out_specs=P(("grp", "loc"), "tp"), check_vma=False
    )
```
